32 devices in a mesh: ctx: 8 (over z, x), tp: 4 (over y, core).
Axes of the slice: x: 2, y: 2, z: 4, core: 2. Of those that a mesh axis runs over, the one named last changes fastest.
Arguments:
- gate_q: bfloat16 [1024, 2048], P('tp', 'ctx'), may hold values from -6 to 6
- key_k: bfloat16 [1024, 2048], P('tp', 'ctx'), may hold values from -6 to 6
- value_v: bfloat16 [1024, 2048], P('tp', 'ctx'), may hold values from -6 to 6
- filter_taps: float32 [1024, 2048], P('tp', 'ctx'), may hold values from -1 to 1
- skip_bias: float32 [1024], P('tp'), may hold values from 0.5 to 1.5
- w_out: bfloat16 [1024, 4096], P('tp'), may hold values from -0.25 to 0.25
Outputs:
- mixed: bfloat16 [4096, 2048], P('tp', 'ctx')
The draws below stay inside these ranges and needn't reach their ends.
All inputs are finite; a program needn't handle non-finite values.
Results may differ from the reference program's by a relative error of at most 0.018.
Values may be sent and summed in bfloat16 or wider, within the bound.
No kernel may reach another device: no remote copies, remote signals or barrier semaphores. Data moves between devices by JAX's collectives and lax.ppermute only.
A program may use at most 64 MiB of HBM per device.

```python
import math
import jax
import jax.numpy as jnp
from jax import lax

CH_DEV = 256
D = 4096
SEQ = 2048
CHANNELS = 1024
N_TP = 4


def draw_filter_taps(key, part):
    key_pick, key_slow, key_fast, key_rough = jax.random.split(key, 4)
    slow_share = 5
    chosen = jax.random.randint(key_pick, (CHANNELS, 1), 0, 10) < slow_share
    slow_tau = SEQ * jnp.exp(jax.random.uniform(key_slow, (CHANNELS, 1), minval=0.0, maxval=math.log(8.0)))
    fast_tau = jax.random.uniform(key_fast, (CHANNELS, 1), minval=30.0, maxval=50.0)
    decay_len = jnp.where(chosen, slow_tau, fast_tau)
    positions = jnp.arange(SEQ, dtype=jnp.float32)[None, :]
    rough = jnp.clip(jax.random.normal(key_rough, (CHANNELS, SEQ)), -4.0, 4.0)
    scale_rows = 1.0 / jnp.sqrt(jnp.minimum(decay_len, SEQ * 1.0))
    return (rough * jnp.exp(-positions / decay_len) * scale_rows).astype(jnp.float32)


def strengthened(result, rng, source, target, blocks, factor):
    def block_of(axis_at):
        return (jnp.arange(result.shape[axis_at]) // (result.shape[axis_at] // blocks)).reshape((-1,) + (1,) * (result.ndim - 1 - axis_at))

    first = jax.random.permutation(rng, blocks)[block_of(target)]
    other_side = (block_of(target) + blocks // 2) % blocks
    return jnp.where((block_of(source) == first) | (block_of(source) == other_side), factor * result, result)


def block_scale(own_key, extent, shards, least, largest):
    loudness, own = 1.0, jax.random.fold_in(own_key, 6)
    for position, shards_of in shards:
        heights = jnp.exp(jax.random.uniform(jax.random.fold_in(own, position), (shards_of,), jnp.float32, least / len(shards), largest / len(shards)))
        loudness = loudness * jnp.repeat(heights, extent[position] // shards_of).reshape([-1 if axis == position else 1 for axis in range(len(extent))])
    return loudness


def bell_draw(stream_key, extent, deviation, most, cuts=(), held_as=jnp.bfloat16):
    array = deviation * jax.random.normal(stream_key, extent, jnp.float32)
    if cuts:
        array = array * block_scale(stream_key, extent, cuts, -0.22, 0.18)
    return jnp.clip(array, -most, most).astype(held_as)


def gaussian_with(stream_key, extent, width, most, cuts, heavy, kind=jnp.bfloat16):
    entries = width * jax.random.normal(stream_key, extent, jnp.float32)
    if cuts:
        entries = entries * block_scale(stream_key, extent, cuts, -0.22, 0.18)
    return jnp.clip(strengthened(entries, jax.random.fold_in(stream_key, 3), *heavy), -most, most).astype(kind)


def setup_inputs(seed: int = 0) -> dict:
    key_of = jax.random.split(jax.random.key(seed), 7)
    gate_q = bell_draw(key_of[0], (CHANNELS, SEQ), 1.0, 6.0, ((0, 4), (1, 8)))
    key_k = bell_draw(key_of[1], (CHANNELS, SEQ), 1.0, 6.0, ((0, 4), (1, 8)))
    value_v = bell_draw(key_of[2], (CHANNELS, SEQ), 1.0, 6.0, ((0, 4), (1, 8)))
    filter_taps = draw_filter_taps(jax.random.fold_in(key_of[6], 71), 0)
    skip_bias = jnp.clip(0.5 + 1.0 * jax.random.uniform(key_of[4], (CHANNELS,), jnp.float32) ** block_scale(key_of[4], (CHANNELS,), ((0, 4),), -0.2, 0.2), 0.5, 1.5)
    w_out = gaussian_with(key_of[5], (CHANNELS, D), CHANNELS ** -0.5, 0.25, ((0, 4),), (0, 1, 4, 2.0))
    return {"gate_q": gate_q, "key_k": key_k, "value_v": value_v, "filter_taps": filter_taps, "skip_bias": skip_bias, "w_out": w_out}


def reference(gate_q, key_k, value_v, filter_taps, skip_bias, w_out):
    length = 2 * SEQ

    def add_block(running, block_id):
        first_row = (block_id * CH_DEV).astype(jnp.int32)
        gate_rows = lax.dynamic_slice_in_dim(gate_q, first_row, CH_DEV, 0).astype(jnp.float32)
        key_rows = lax.dynamic_slice_in_dim(key_k, first_row, CH_DEV, 0).astype(jnp.float32)
        value_rows = lax.dynamic_slice_in_dim(value_v, first_row, CH_DEV, 0).astype(jnp.float32)
        tap_rows = lax.dynamic_slice_in_dim(filter_taps, first_row, CH_DEV, 0)
        bias_rows = lax.dynamic_slice_in_dim(skip_bias, first_row, CH_DEV, 0)
        weight = lax.dynamic_slice_in_dim(w_out, first_row, CH_DEV, 0)
        signal = key_rows * value_rows
        spectrum = jnp.fft.rfft(signal, n=length, axis=1) * jnp.fft.rfft(tap_rows, n=length, axis=1)
        convolved = jnp.fft.irfft(spectrum, n=length, axis=1)[:, :SEQ]
        gated_vals = (gate_rows * (convolved + bias_rows[:, None] * signal)).astype(jnp.bfloat16)
        partial_value = lax.dot_general(weight, gated_vals, (((0,), (0,)), ((), ())), preferred_element_type=jnp.float32)
        partial_value = partial_value.astype(jnp.bfloat16)
        return running + partial_value.astype(jnp.float32), None

    running, _ = lax.scan(add_block, jnp.zeros((D, SEQ), jnp.float32), jnp.arange(N_TP, dtype=jnp.int32))
    return running.astype(jnp.bfloat16)
```

```python
import jax
import jax.numpy as jnp
from jax import lax
from jax.experimental import pallas as pl
from jax.experimental.pallas import tpu as pltpu
from jax.sharding import PartitionSpec as P

LANES = 128
PACK = 16
SUB = 64
PHASES = LANES // SUB


def conv_kernel(x_ref, y_ref, taps, rows, sums):
    blocks, _, chans, seq_dev = x_ref.shape
    halves = seq_dev // LANES
    lines = blocks * halves
    length = lines * LANES
    lane = lax.broadcasted_iota(jnp.int32, (chans, LANES), 1)

    taps[:, pl.ds(0, LANES)] = jnp.zeros((chans, LANES), jnp.float32)
    zero = jnp.zeros((chans * lines, LANES), jnp.float32)
    for phase in range(PHASES):
        for chan in range(chans):
            rows[phase, pl.ds(chan * 2 * lines, lines), :] = jnp.zeros((lines, LANES), jnp.float32)
    del zero
    older = [jnp.zeros((chans, LANES), jnp.float32)] * (PHASES - 1)
    for line in range(lines):
        block, half = divmod(line, halves)
        cut = pl.ds(half * LANES, LANES)
        taps[:, pl.ds(LANES + line * LANES, LANES)] = x_ref[block, 1, :, cut].astype(jnp.float32)
        now = [x_ref[block, 0, :, cut].astype(jnp.float32)] + older
        older = now[: PHASES - 1]
        for phase in range(PHASES):
            made = None
            for step in range(PHASES):
                turn = (SUB * (step - phase)) % LANES
                piece = pltpu.roll(now[step], turn, axis=1) if turn else now[step]
                made = piece if made is None else jnp.where(lane >= SUB * step, piece, made)
            rows[phase, pl.ds(lines + line, chans, stride=2 * lines), :] = made

    def channel(chan, _):
        wide = jnp.broadcast_to(taps[pl.ds(chan, 1), :], (PACK, LANES + length))
        skew = pltpu.roll(wide, 0, 1, stride=1, stride_axis=0).astype(jnp.bfloat16)
        parts = []
        for part in range(SUB // PACK):
            parts.append(pltpu.roll(skew, part * PACK, 1) if part else skew)
        toeplitz = jnp.concatenate(
            [part[:, (line + 1) * LANES : (line + 2) * LANES] for line in range(lines) for part in parts], 0
        )
        base = chan * 2 * lines + lines
        left = jnp.concatenate(
            [
                jnp.concatenate(
                    [
                        rows[phase, pl.ds(base - PHASES * step, lines), :].astype(jnp.bfloat16)
                        for step in range(lines // PHASES)
                    ],
                    1,
                )
                for phase in range(PHASES)
            ],
            0,
        )
        total = jnp.dot(left, toeplitz, preferred_element_type=jnp.float32)
        for phase in range(PHASES):
            sums[phase, pl.ds(chan * lines, lines), :] = total[phase * lines : (phase + 1) * lines]
        return 0

    lax.fori_loop(0, chans, channel, 0)

    older = [jnp.zeros((chans, LANES), jnp.float32)] * PHASES
    for line in range(lines):
        block, half = divmod(line, halves)
        now = [sums[phase, pl.ds(line, chans, stride=lines), :] for phase in range(PHASES)]
        value = now[0]
        for phase in range(1, PHASES):
            mixed = jnp.where(lane < LANES - SUB * phase, now[phase], older[phase])
            value = value + pltpu.roll(mixed, SUB * phase, axis=1)
        older = now
        y_ref[block, :, pl.ds(half * LANES, LANES)] = value.astype(jnp.bfloat16)


def convolve(pieces):
    blocks, _, chans, seq_dev = pieces.shape
    lines = blocks * seq_dev // LANES
    return pl.pallas_call(
        conv_kernel,
        out_shape=jax.ShapeDtypeStruct((blocks, chans, seq_dev), jnp.bfloat16),
        in_specs=[pl.BlockSpec(memory_space=pltpu.VMEM)],
        out_specs=pl.BlockSpec(memory_space=pltpu.VMEM),
        scratch_shapes=[
            pltpu.VMEM((chans, LANES + lines * LANES), jnp.float32),
            pltpu.VMEM((PHASES, chans * 2 * lines, LANES), jnp.float32),
            pltpu.VMEM((PHASES, chans * lines, LANES), jnp.float32),
        ],
        compiler_params=pltpu.CompilerParams(vmem_limit_bytes=40 * 2**20),
        cost_estimate=pl.CostEstimate(
            flops=2 * chans * lines * LANES * lines * LANES,
            bytes_accessed=6 * chans * lines * LANES,
            transcendentals=0,
        ),
        name="toeplitz_conv",
    )(pieces)


def body(gate_q, key_k, value_v, filter_taps, skip_bias, w_out):
    channels, seq_dev = key_k.shape
    shards = lax.axis_size("ctx")
    tp = lax.axis_size("tp")
    me = lax.axis_index("tp")
    share = channels // shards
    feats = w_out.shape[1] // tp
    signal = key_k.astype(jnp.float32) * value_v.astype(jnp.float32)
    pieces = jnp.stack(
        [
            signal.astype(jnp.bfloat16).reshape(shards, share, seq_dev),
            filter_taps.astype(jnp.bfloat16).reshape(shards, share, seq_dev),
        ],
        1,
    )

    def own_feats(owner):
        return lax.dynamic_slice_in_dim(w_out, owner * feats, feats, 1)

    weights = [own_feats(me)]
    for step in range(1, tp):
        weights.append(lax.ppermute(own_feats((me + step) % tp), "tp", [(i, (i + step) % tp) for i in range(tp)]))

    pieces = lax.all_to_all(pieces, "ctx", split_axis=0, concat_axis=0, tiled=True)
    convolved = convolve(pieces)
    convolved = lax.all_to_all(convolved, "ctx", split_axis=0, concat_axis=0, tiled=True)
    convolved, *weights = lax.optimization_barrier((convolved, *weights))
    convolved = convolved.reshape(channels, seq_dev).astype(jnp.float32)
    gated_vals = (gate_q.astype(jnp.float32) * (convolved + skip_bias[:, None] * signal)).astype(jnp.bfloat16)
    gathered = lax.all_gather(gated_vals, "tp", axis=0, tiled=True)
    total = None
    for step in range(tp):
        rows = lax.dynamic_slice_in_dim(gathered, ((me - step) % tp) * channels, channels, 0)
        term = lax.dot_general(weights[step], rows, (((0,), (0,)), ((), ())), preferred_element_type=jnp.float32)
        total = term if total is None else total + term
    return total.astype(jnp.bfloat16)


def solution(mesh):
    return jax.shard_map(
        body,
        mesh=mesh,
        in_specs=(P("tp", "ctx"), P("tp", "ctx"), P("tp", "ctx"), P("tp", "ctx"), P("tp"), P("tp", None)),
        out_specs=P("tp", "ctx"),
        check_vma=False,
    )
```

```python
import jax
import jax.numpy as jnp
from jax import lax
from jax.experimental import pallas as pl
from jax.experimental.pallas import tpu as pltpu
from jax.sharding import PartitionSpec as P

LANES = 128
PACK = 16
SUB = 32
PHASES = LANES // SUB


def conv_kernel(x_ref, y_ref, taps, rows, sums):
    blocks, _, chans, seq_dev = x_ref.shape
    halves = seq_dev // LANES
    lines = blocks * halves
    length = lines * LANES
    lane = lax.broadcasted_iota(jnp.int32, (chans, LANES), 1)

    taps[:, pl.ds(0, LANES)] = jnp.zeros((chans, LANES), jnp.float32)
    zero = jnp.zeros((chans * lines, LANES), jnp.float32)
    for phase in range(PHASES):
        for chan in range(chans):
            rows[phase, pl.ds(chan * 2 * lines, lines), :] = jnp.zeros((lines, LANES), jnp.float32)
    del zero
    older = [jnp.zeros((chans, LANES), jnp.float32)] * (PHASES - 1)
    for line in range(lines):
        block, half = divmod(line, halves)
        cut = pl.ds(half * LANES, LANES)
        taps[:, pl.ds(LANES + line * LANES, LANES)] = x_ref[block, 1, :, cut].astype(jnp.float32)
        now = [x_ref[block, 0, :, cut].astype(jnp.float32)] + older
        older = now[: PHASES - 1]
        for phase in range(PHASES):
            made = None
            for step in range(PHASES):
                turn = (SUB * (step - phase)) % LANES
                piece = pltpu.roll(now[step], turn, axis=1) if turn else now[step]
                made = piece if made is None else jnp.where(lane >= SUB * step, piece, made)
            rows[phase, pl.ds(lines + line, chans, stride=2 * lines), :] = made

    def channel(chan, _):
        wide = jnp.broadcast_to(taps[pl.ds(chan, 1), :], (PACK, LANES + length))
        skew = pltpu.roll(wide, 0, 1, stride=1, stride_axis=0).astype(jnp.bfloat16)
        parts = []
        for part in range(SUB // PACK):
            parts.append(pltpu.roll(skew, part * PACK, 1) if part else skew)
        toeplitz = jnp.concatenate(
            [part[:, (line + 1) * LANES : (line + 2) * LANES] for line in range(lines) for part in parts], 0
        )
        base = chan * 2 * lines + lines
        left = jnp.concatenate(
            [
                jnp.concatenate(
                    [
                        rows[phase, pl.ds(base - PHASES * step, lines), :].astype(jnp.bfloat16)
                        for step in range(lines // PHASES)
                    ],
                    1,
                )
                for phase in range(PHASES)
            ],
            0,
        )
        total = jnp.dot(left, toeplitz, preferred_element_type=jnp.float32)
        for phase in range(PHASES):
            sums[phase, pl.ds(chan * lines, lines), :] = total[phase * lines : (phase + 1) * lines]
        return 0

    lax.fori_loop(0, chans, channel, 0, unroll=8 if chans % 8 == 0 else 1)

    older = [jnp.zeros((chans, LANES), jnp.float32)] * PHASES
    for line in range(lines):
        block, half = divmod(line, halves)
        now = [sums[phase, pl.ds(line, chans, stride=lines), :] for phase in range(PHASES)]
        value = now[0]
        for phase in range(1, PHASES):
            mixed = jnp.where(lane < LANES - SUB * phase, now[phase], older[phase])
            value = value + pltpu.roll(mixed, SUB * phase, axis=1)
        older = now
        y_ref[block, :, pl.ds(half * LANES, LANES)] = value.astype(jnp.bfloat16)


def convolve(pieces):
    blocks, _, chans, seq_dev = pieces.shape
    lines = blocks * seq_dev // LANES
    return pl.pallas_call(
        conv_kernel,
        out_shape=jax.ShapeDtypeStruct((blocks, chans, seq_dev), jnp.bfloat16),
        in_specs=[pl.BlockSpec(memory_space=pltpu.VMEM)],
        out_specs=pl.BlockSpec(memory_space=pltpu.VMEM),
        scratch_shapes=[
            pltpu.VMEM((chans, LANES + lines * LANES), jnp.float32),
            pltpu.VMEM((PHASES, chans * 2 * lines, LANES), jnp.float32),
            pltpu.VMEM((PHASES, chans * lines, LANES), jnp.float32),
        ],
        compiler_params=pltpu.CompilerParams(vmem_limit_bytes=40 * 2**20),
        cost_estimate=pl.CostEstimate(flops=1, bytes_accessed=1, transcendentals=0),
        name="toeplitz_conv",
    )(pieces)


def partner(me, step, tp):
    if tp & (tp - 1) == 0:
        return me ^ step
    return (me + step) % tp


def source(me, step, tp):
    if tp & (tp - 1) == 0:
        return me ^ step
    return (me + tp - step) % tp


def exchanges(tp, channels):
    early = tp // 2
    return [(step, 0, channels) for step in [early] + [step for step in range(tp - 1, 0, -1) if step != early]]


def prepare_kernel(key_ref, value_ref, taps_ref, w_ref, pieces_ref, *refs):
    shards, _, share, _ = pieces_ref.shape
    tp = lax.axis_size("tp")
    feats = w_ref.shape[1] // tp
    me = lax.axis_index("tp")
    plan = exchanges(tp, w_ref.shape[0])
    cuts, (key, value, taps, in_sems, sems) = refs[: len(plan)], refs[len(plan) :]
    loads = []
    for place, (ref, held) in enumerate(((key_ref, key), (value_ref, value), (taps_ref, taps))):
        loads.append(pltpu.make_async_copy(ref, held, in_sems.at[place]))
        loads[-1].start()
    copies = []
    for place, (step, first, count) in enumerate(plan):
        column = pl.multiple_of(partner(me, step, tp) * feats, LANES)
        cut = w_ref.at[pl.ds(first, count), pl.ds(column, feats)]
        copies.append(pltpu.make_async_copy(cut, cuts[place], sems.at[place]))
        copies[-1].start()
    for load in loads:
        load.wait()
    for shard in range(shards):
        rows = pl.ds(shard * share, share)
        signal = key[rows, :].astype(jnp.float32) * value[rows, :].astype(jnp.float32)
        pieces_ref[shard, 0] = signal.astype(jnp.bfloat16)
        pieces_ref[shard, 1] = taps[rows, :].astype(jnp.bfloat16)
    for copy in copies:
        copy.wait()


def prepare(key_k, value_v, filter_taps, w_out, shards, tp):
    channels, seq_dev = key_k.shape
    feats = w_out.shape[1] // tp
    plan = exchanges(tp, channels)
    vmem, hbm = pl.BlockSpec(memory_space=pltpu.VMEM), pl.BlockSpec(memory_space=pltpu.HBM)
    return pl.pallas_call(
        prepare_kernel,
        out_shape=[jax.ShapeDtypeStruct((shards, 2, channels // shards, seq_dev), jnp.bfloat16)]
        + [jax.ShapeDtypeStruct((count, feats), jnp.bfloat16) for _, _, count in plan],
        in_specs=[hbm, hbm, hbm, hbm],
        out_specs=[vmem] * (1 + len(plan)),
        scratch_shapes=[
            pltpu.VMEM(key_k.shape, key_k.dtype),
            pltpu.VMEM(value_v.shape, value_v.dtype),
            pltpu.VMEM(filter_taps.shape, filter_taps.dtype),
            pltpu.SemaphoreType.DMA((3,)),
            pltpu.SemaphoreType.DMA((len(plan),)),
        ],
        compiler_params=pltpu.CompilerParams(vmem_limit_bytes=60 * 2**20),
        cost_estimate=pl.CostEstimate(flops=channels * seq_dev, bytes_accessed=4 * w_out.size, transcendentals=0),
        name="prepare",
    )(key_k, value_v, filter_taps, w_out)


def project_kernel(gated_ref, own_ref, *refs):
    weights, out_ref = refs[:-1], refs[-1]
    tp = lax.axis_size("tp")
    channels = own_ref.shape[0]
    me = lax.axis_index("tp")

    def term(weight_ref, step, first, count):
        row = pl.multiple_of(source(me, step, tp) * channels + first, PACK)
        return lax.dot_general(
            weight_ref[...],
            gated_ref[pl.ds(row, count), :],
            (((0,), (0,)), ((), ())),
            preferred_element_type=jnp.float32,
        )

    total = term(own_ref, 0, 0, channels)
    for weight_ref, (step, first, count) in zip(weights, exchanges(tp, channels)):
        total = total + term(weight_ref, step, first, count)
    out_ref[...] = total.astype(jnp.bfloat16)


def project(gathered, own, weights):
    channels, feats = own.shape
    rows, seq_dev = gathered.shape
    return pl.pallas_call(
        project_kernel,
        out_shape=jax.ShapeDtypeStruct((feats, seq_dev), jnp.bfloat16),
        in_specs=[pl.BlockSpec(memory_space=pltpu.VMEM)] * (2 + len(weights)),
        out_specs=pl.BlockSpec(memory_space=pltpu.VMEM),
        compiler_params=pltpu.CompilerParams(vmem_limit_bytes=24 * 2**20),
        cost_estimate=pl.CostEstimate(
            flops=2 * rows * feats * seq_dev, bytes_accessed=2 * rows * (feats + seq_dev), transcendentals=0
        ),
        name="project",
    )(gathered, own, *weights)


def body(gate_q, key_k, value_v, filter_taps, skip_bias, w_out):
    channels, seq_dev = key_k.shape
    shards = lax.axis_size("ctx")
    tp = lax.axis_size("tp")
    me = lax.axis_index("tp")
    feats = w_out.shape[1] // tp
    pieces, *cuts = prepare(key_k, value_v, filter_taps, w_out, shards, tp)
    weights = [
        lax.ppermute(cut, "tp", [(i, partner(i, step, tp)) for i in range(tp)])
        for cut, (step, _, _) in zip(cuts, exchanges(tp, channels))
    ]
    pieces = lax.all_to_all(pieces, "ctx", split_axis=0, concat_axis=0, tiled=True)
    convolved = convolve(pieces)
    convolved, weights[0] = lax.optimization_barrier((convolved, weights[0]))
    convolved = lax.all_to_all(convolved, "ctx", split_axis=0, concat_axis=0, tiled=True)
    own = lax.dynamic_slice_in_dim(w_out, me * feats, feats, 1)
    convolved, own, *weights = lax.optimization_barrier((convolved, own, *weights))
    convolved = convolved.reshape(channels, seq_dev).astype(jnp.float32)
    signal = key_k.astype(jnp.float32) * value_v.astype(jnp.float32)
    gated_vals = (gate_q.astype(jnp.float32) * (convolved + skip_bias[:, None] * signal)).astype(jnp.bfloat16)
    gathered = lax.all_gather(gated_vals, "tp", axis=0, tiled=True)
    return project(gathered, own, weights)


def solution(mesh):
    return jax.shard_map(
        body,
        mesh=mesh,
        in_specs=(P("tp", "ctx"), P("tp", "ctx"), P("tp", "ctx"), P("tp", "ctx"), P("tp"), P("tp", None)),
        out_specs=P("tp", "ctx"),
        check_vma=False,
    )
```

```python
import jax
import jax.numpy as jnp
from jax import lax
from jax.experimental import pallas as pl
from jax.experimental.pallas import tpu as pltpu
from jax.sharding import PartitionSpec as P

LANES = 128
PACK = 16
SUB = 16
PHASES = LANES // SUB
CORES = 2


def pitches(lines):
    pad = lines - PHASES
    return pad, (pad + lines) | 1, lines | 1


def conv_kernel(x_ref, bias_ref, y_ref, taps, rows, sums):
    blocks, _, chans, seq_dev = x_ref.shape
    halves = seq_dev // LANES
    lines = blocks * halves
    length = lines * LANES
    lane = lax.broadcasted_iota(jnp.int32, (chans, LANES), 1)

    taps[:, pl.ds(0, LANES)] = jnp.zeros((chans, LANES), jnp.float32)
    pad, row_pitch, sum_pitch = pitches(lines)
    for phase in range(PHASES):
        for chan in range(chans):
            rows[phase, pl.ds(chan * row_pitch, pad), :] = jnp.zeros((pad, LANES), jnp.float32)
    older = [[jnp.zeros((chans, LANES), jnp.float32)] * PHASES] * (PHASES - 1)
    for line in range(lines):
        block, half = divmod(line, halves)
        cut = pl.ds(half * LANES, LANES)
        taps[:, pl.ds(LANES + line * LANES, LANES)] = x_ref[block, 1, :, cut].astype(jnp.float32)
        fresh = x_ref[block, 0, :, cut].astype(jnp.float32)
        now = [[fresh] + [pltpu.roll(fresh, SUB * turn, axis=1) for turn in range(1, PHASES)]] + older
        older = now[: PHASES - 1]
        for phase in range(PHASES):
            made = now[0][-phase % PHASES]
            for step in range(1, PHASES):
                made = jnp.where(lane >= SUB * step, now[step][(step - phase) % PHASES], made)
            rows[phase, pl.ds(pad + line, chans, stride=row_pitch), :] = made

    def channel(chan, _):
        wide = jnp.broadcast_to(taps[pl.ds(chan, 1), :], (PACK, LANES + length))
        skew = pltpu.roll(wide, 0, 1, stride=1, stride_axis=0).astype(jnp.bfloat16)
        parts = []
        for part in range(SUB // PACK):
            parts.append(pltpu.roll(skew, part * PACK, 1) if part else skew)
        toeplitz = jnp.concatenate(
            [part[:, (line + 1) * LANES : (line + 2) * LANES] for line in range(lines) for part in parts], 0
        )
        base = chan * row_pitch + pad
        left = jnp.concatenate(
            [
                jnp.concatenate(
                    [
                        rows[phase, pl.ds(base - PHASES * step, lines), :].astype(jnp.bfloat16)
                        for step in range(lines // PHASES)
                    ],
                    1,
                )
                for phase in range(PHASES)
            ],
            0,
        )
        total = jnp.dot(left, toeplitz, preferred_element_type=jnp.float32)
        for phase in range(PHASES):
            sums[phase, pl.ds(chan * sum_pitch, lines), :] = total[phase * lines : (phase + 1) * lines]
        return 0

    lax.fori_loop(0, chans, channel, 0, unroll=16 if chans % 16 == 0 else 1)

    first = pl.multiple_of(lax.axis_index("ctx") * chans, chans)
    bias = jnp.broadcast_to(bias_ref[pl.ds(first, chans), :], (chans, LANES))
    older = [jnp.zeros((chans, LANES), jnp.float32)] * PHASES
    for line in range(lines):
        block, half = divmod(line, halves)
        now = [sums[phase, pl.ds(line, chans, stride=sum_pitch), :] for phase in range(PHASES)]
        cut = pl.ds(half * LANES, LANES)
        value = now[0] + bias * x_ref[block, 0, :, cut].astype(jnp.float32)
        for phase in range(1, PHASES):
            mixed = jnp.where(lane < LANES - SUB * phase, now[phase], older[phase])
            value = value + pltpu.roll(mixed, SUB * phase, axis=1)
        older = now
        for copy in range(y_ref.shape[1]):
            y_ref[block, copy, :, cut] = value.astype(jnp.bfloat16)


def convolve(pieces, bias, copies):
    blocks, _, chans, seq_dev = pieces.shape
    lines = blocks * seq_dev // LANES
    _, row_pitch, sum_pitch = pitches(lines)
    return pl.pallas_call(
        conv_kernel,
        out_shape=jax.ShapeDtypeStruct((blocks, copies, chans, seq_dev), jnp.bfloat16),
        in_specs=[pl.BlockSpec(memory_space=pltpu.VMEM)] * 2,
        out_specs=pl.BlockSpec(memory_space=pltpu.VMEM),
        scratch_shapes=[
            pltpu.VMEM((chans, LANES + lines * LANES), jnp.float32),
            pltpu.VMEM((PHASES, chans * row_pitch, LANES), jnp.float32),
            pltpu.VMEM((PHASES, chans * sum_pitch, LANES), jnp.float32),
        ],
        compiler_params=pltpu.CompilerParams(vmem_limit_bytes=16 * 2**20),
        cost_estimate=pl.CostEstimate(flops=1, bytes_accessed=1, transcendentals=0),
        name="toeplitz_conv",
    )(pieces, bias)


def partner(me, step, tp):
    chips, other = step
    return (me // CORES + chips) % (tp // CORES) * CORES + (me % CORES + other) % CORES


def source(me, step, tp):
    chips, other = step
    return (me // CORES + tp // CORES - chips) % (tp // CORES) * CORES + (me % CORES + CORES - other) % CORES


def exchanges(tp):
    steps = [(chips, other) for chips in range(tp // CORES) for other in range(CORES)][1:]
    early = (tp // CORES // 2, 0)
    return [early] + [step for step in reversed(steps) if step != early]


def prepare_kernel(key_ref, value_ref, taps_ref, w_ref, pieces_ref, *refs):
    shards, _, share, _ = pieces_ref.shape
    tp = lax.axis_size("tp")
    feats = w_ref.shape[1] // tp
    me = lax.axis_index("tp")
    plan = exchanges(tp)[: len(refs) - 5]
    cuts, (key, value, taps, in_sems, sems) = refs[: len(plan)], refs[len(plan) :]
    loads = []
    for place, (ref, held) in enumerate(((key_ref, key), (value_ref, value), (taps_ref, taps))):
        loads.append(pltpu.make_async_copy(ref, held, in_sems.at[place]))
        loads[-1].start()
    copies = []
    for place, step in enumerate(plan):
        column = pl.multiple_of(partner(me, step, tp) * feats, LANES)
        cut = w_ref.at[:, pl.ds(column, feats)]
        copies.append(pltpu.make_async_copy(cut, cuts[place], sems.at[place]))
        copies[-1].start()
    for load in loads:
        load.wait()
    for shard in range(shards):
        rows = pl.ds(shard * share, share)
        signal = key[rows, :].astype(jnp.float32) * value[rows, :].astype(jnp.float32)
        pieces_ref[shard, 0] = signal.astype(jnp.bfloat16)
        pieces_ref[shard, 1] = taps[rows, :].astype(jnp.bfloat16)
    for copy in copies:
        copy.wait()


def prepare(key_k, value_v, filter_taps, w_out, shards, tp):
    channels, seq_dev = key_k.shape
    feats = w_out.shape[1] // tp
    plan = exchanges(tp)[:1]
    vmem, hbm = pl.BlockSpec(memory_space=pltpu.VMEM), pl.BlockSpec(memory_space=pltpu.HBM)
    return pl.pallas_call(
        prepare_kernel,
        out_shape=[pltpu.VMEM((shards, 2, channels // shards, seq_dev), jnp.bfloat16)]
        + [pltpu.VMEM((channels, feats), jnp.bfloat16)] * len(plan),
        in_specs=[hbm, hbm, hbm, hbm],
        out_specs=[vmem] * (1 + len(plan)),
        scratch_shapes=[
            pltpu.VMEM(key_k.shape, key_k.dtype),
            pltpu.VMEM(value_v.shape, value_v.dtype),
            pltpu.VMEM(filter_taps.shape, filter_taps.dtype),
            pltpu.SemaphoreType.DMA((3,)),
            pltpu.SemaphoreType.DMA((len(plan),)),
        ],
        compiler_params=pltpu.CompilerParams(vmem_limit_bytes=8 * 2**20),
        cost_estimate=pl.CostEstimate(flops=channels * seq_dev, bytes_accessed=4 * w_out.size, transcendentals=0),
        name="prepare",
    )(*(pltpu.with_memory_space_constraint(x, pltpu.HBM) for x in (key_k, value_v, filter_taps, w_out)))


def gate_kernel(conv_ref, *refs):
    gates, out_ref = refs[:-1], refs[-1]
    blocks, chips, share, _ = conv_ref.shape
    channels = blocks * share
    row = lax.axis_index("tp") // CORES
    for step, gate_ref in enumerate(gates):
        other = (row + chips - step) % chips
        for block in range(blocks):
            rows = pl.ds(block * share, share)
            gated = gate_ref[rows, :].astype(jnp.float32) * conv_ref[block, other].astype(jnp.float32)
            out_ref[pl.ds(step * channels + block * share, share), :] = gated.astype(jnp.bfloat16)


def gate(convolved, gates):
    blocks, chips, share, seq_dev = convolved.shape
    return pl.pallas_call(
        gate_kernel,
        out_shape=pltpu.VMEM((chips * blocks * share, seq_dev), jnp.bfloat16),
        in_specs=[pl.BlockSpec(memory_space=pltpu.VMEM)] * (1 + chips),
        out_specs=pl.BlockSpec(memory_space=pltpu.VMEM),
        compiler_params=pltpu.CompilerParams(vmem_limit_bytes=8 * 2**20),
        name="gate",
    )(convolved, *(pltpu.with_memory_space_constraint(x, pltpu.VMEM) for x in gates))


def project_kernel(gated_ref, own_ref, *refs):
    weights, out_ref = (own_ref, *refs[:-1]), refs[-1]
    tp = lax.axis_size("tp")
    channels = own_ref.shape[0]
    core = lax.axis_index("tp") % CORES
    total = None
    for weight_ref, (chips, other) in zip(weights, [(0, 0)] + exchanges(tp)):
        place = (core + CORES - other) % CORES * (tp // CORES) + chips
        term = lax.dot_general(
            weight_ref[...],
            gated_ref[pl.ds(pl.multiple_of(place * channels, channels), channels), :],
            (((0,), (0,)), ((), ())),
            preferred_element_type=jnp.float32,
        )
        total = term if total is None else total + term
    out_ref[...] = total.astype(jnp.bfloat16)


def project(gathered, own, weights):
    channels, feats = own.shape
    rows, seq_dev = gathered.shape
    return pl.pallas_call(
        project_kernel,
        out_shape=jax.ShapeDtypeStruct((feats, seq_dev), jnp.bfloat16),
        in_specs=[pl.BlockSpec(memory_space=pltpu.VMEM)] * (2 + len(weights)),
        out_specs=pl.BlockSpec(memory_space=pltpu.VMEM),
        compiler_params=pltpu.CompilerParams(vmem_limit_bytes=24 * 2**20),
        cost_estimate=pl.CostEstimate(
            flops=2 * rows * feats * seq_dev, bytes_accessed=2 * rows * (feats + seq_dev), transcendentals=0
        ),
        name="project",
    )(gathered, own, *weights)


def body(gate_q, key_k, value_v, filter_taps, skip_bias, w_out):
    channels, seq_dev = key_k.shape
    shards = lax.axis_size("ctx")
    tp = lax.axis_size("tp")
    me = lax.axis_index("tp")
    chips = tp // CORES
    feats = w_out.shape[1] // tp

    def exchange(array, step):
        return lax.ppermute(array, "tp", [(i, partner(i, step, tp)) for i in range(tp)])

    pieces, *cuts = prepare(key_k, value_v, filter_taps, w_out, shards, tp)
    for step in exchanges(tp)[len(cuts) :]:
        cuts.append(lax.dynamic_slice_in_dim(w_out, partner(me, step, tp) * feats, feats, 1))
    weights = [exchange(cut, step) for cut, step in zip(cuts, exchanges(tp))]
    gates = [gate_q] + [exchange(gate_q, (step, 0)) for step in range(1, chips)]

    pieces = lax.all_to_all(pieces, "ctx", split_axis=0, concat_axis=0, tiled=True)
    convolved = convolve(pieces, skip_bias.reshape(channels, 1), chips)
    convolved, weights[0] = lax.optimization_barrier((convolved, weights[0]))
    convolved = lax.all_to_all(
        convolved.reshape(shards * chips, channels // shards, seq_dev),
        ("ctx", "tp"),
        split_axis=0,
        concat_axis=0,
        tiled=True,
        axis_index_groups=[
            [shard * tp + chip * CORES + core for shard in range(shards) for chip in range(chips)] for core in range(CORES)
        ],
    )
    own = lax.dynamic_slice_in_dim(w_out, me * feats, feats, 1)
    convolved, own, gates, weights = lax.optimization_barrier((convolved, own, gates, weights))
    gated_vals = gate(convolved.reshape(shards, chips, channels // shards, seq_dev), gates)
    gathered = lax.all_gather(
        gated_vals,
        "tp",
        axis=0,
        tiled=True,
        axis_index_groups=[[chip * CORES + core for core in range(CORES)] for chip in range(chips)],
    )
    return project(gathered, own, weights)


def solution(mesh):
    return jax.shard_map(
        body,
        mesh=mesh,
        in_specs=(P("tp", "ctx"), P("tp", "ctx"), P("tp", "ctx"), P("tp", "ctx"), P("tp"), P("tp", None)),
        out_specs=P("tp", "ctx"),
        check_vma=False,
    )
```

```python
import jax
import jax.numpy as jnp
from jax import lax
from jax.experimental import pallas as pl
from jax.experimental.pallas import tpu as pltpu
from jax.sharding import PartitionSpec as P

LANES = 128
PACK = 16
SUB = 16
PHASES = LANES // SUB
CORES = 2


def pitches(lines):
    pad = lines - PHASES
    return pad, (pad + lines) | 1, lines | 1


def conv_kernel(x_ref, bias_ref, y_ref, taps, rows, sums, result, sems):
    blocks, _, chans, seq_dev = x_ref.shape
    halves = seq_dev // LANES
    lines = blocks * halves
    length = lines * LANES
    pad, row_pitch, sum_pitch = pitches(lines)

    taps[:, pl.ds(0, LANES)] = jnp.zeros((chans, LANES), jnp.float32)
    for phase in range(PHASES):
        for chan in range(chans):
            rows[phase, pl.ds(chan * row_pitch, pad), :] = jnp.zeros((pad, LANES), jnp.float32)
    size = 8 if chans % 8 == 0 else chans
    lane = lax.broadcasted_iota(jnp.int32, (size, LANES), 1)
    bits = PHASES.bit_length() - 1
    odd = [lane // (SUB << bit) % 2 == 1 for bit in range(bits)]
    for begin in range(0, chans, size):
        history = [[[jnp.zeros((size, LANES), jnp.float32)] * PHASES] * (1 << bit) for bit in range(bits)]
        for line in range(lines):
            block, half = divmod(line, halves)
            fresh = x_ref[block, 0, pl.ds(begin, size), pl.ds(half * LANES, LANES)].astype(jnp.float32)
            level = [fresh] + [pltpu.roll(fresh, SUB * turn, axis=1) for turn in range(1, PHASES)]
            for bit in range(bits):
                step = 1 << bit
                past = history[bit][0]
                history[bit] = history[bit][1:] + [level]
                level = [jnp.where(odd[bit], past[(turn + step) % PHASES], level[turn]) for turn in range(PHASES)]
            for phase in range(PHASES):
                rows[phase, pl.ds(begin * row_pitch + pad + line, size, stride=row_pitch), :] = level[-phase % PHASES]
    for line in range(lines):
        block, half = divmod(line, halves)
        taps[:, pl.ds(LANES + line * LANES, LANES)] = x_ref[block, 1, :, pl.ds(half * LANES, LANES)].astype(jnp.float32)

    def channel(chan, _):
        wide = jnp.broadcast_to(taps[pl.ds(chan, 1), :], (PACK, LANES + length))
        skew = pltpu.roll(wide, 0, 1, stride=1, stride_axis=0).astype(jnp.bfloat16)
        toeplitz = jnp.concatenate([skew[:, (line + 1) * LANES : (line + 2) * LANES] for line in range(lines)], 0)
        base = chan * row_pitch + pad
        left = jnp.concatenate(
            [
                jnp.concatenate(
                    [
                        rows[phase, pl.ds(base - PHASES * step, lines), :].astype(jnp.bfloat16)
                        for step in range(lines // PHASES)
                    ],
                    1,
                )
                for phase in range(PHASES)
            ],
            0,
        )
        total = jnp.dot(left, toeplitz, preferred_element_type=jnp.float32)
        for phase in range(PHASES):
            sums[phase, pl.ds(chan * sum_pitch, lines), :] = total[phase * lines : (phase + 1) * lines]
        return 0

    lax.fori_loop(0, chans, channel, 0, unroll=True)

    first = pl.multiple_of(lax.axis_index("ctx") * chans, chans)
    size = PACK if chans % PACK == 0 else chans
    lane = lax.broadcasted_iota(jnp.int32, (size, LANES), 1)
    copies = []
    for begin in range(0, chans, size):
        part = pl.ds(begin, size)
        bias = jnp.broadcast_to(bias_ref[pl.ds(first + begin, size), :], (size, LANES))
        older = [jnp.zeros((size, LANES), jnp.float32)] * PHASES
        for line in range(lines):
            block, half = divmod(line, halves)
            cut = pl.ds(half * LANES, LANES)
            now = [sums[phase, pl.ds(begin * sum_pitch + line, size, stride=sum_pitch), :] for phase in range(PHASES)]
            value = now[0] + bias * x_ref[block, 0, part, cut].astype(jnp.float32)
            for phase in range(1, PHASES):
                mixed = jnp.where(lane < LANES - SUB * phase, now[phase], older[phase])
                value = value + pltpu.roll(mixed, SUB * phase, axis=1)
            older = now
            result[block, part, cut] = value.astype(jnp.bfloat16)
        for copy in range(y_ref.shape[1]):
            sem = sems.at[begin // size, copy]
            copies.append(pltpu.make_async_copy(result.at[:, part, :], y_ref.at[:, copy, part, :], sem))
            copies[-1].start()
    for copy in copies:
        copy.wait()


def convolve(pieces, bias, copies):
    blocks, _, chans, seq_dev = pieces.shape
    lines = blocks * seq_dev // LANES
    _, row_pitch, sum_pitch = pitches(lines)
    return pl.pallas_call(
        conv_kernel,
        out_shape=jax.ShapeDtypeStruct((blocks, copies, chans, seq_dev), jnp.bfloat16),
        in_specs=[pl.BlockSpec(memory_space=pltpu.VMEM)] * 2,
        out_specs=pl.BlockSpec(memory_space=pltpu.HBM),
        scratch_shapes=[
            pltpu.VMEM((chans, LANES + lines * LANES), jnp.float32),
            pltpu.VMEM((PHASES, chans * row_pitch, LANES), jnp.float32),
            pltpu.VMEM((PHASES, chans * sum_pitch, LANES), jnp.float32),
            pltpu.VMEM((blocks, chans, seq_dev), jnp.bfloat16),
            pltpu.SemaphoreType.DMA((pl.cdiv(chans, PACK), copies)),
        ],
        compiler_params=pltpu.CompilerParams(vmem_limit_bytes=16 * 2**20),
        cost_estimate=pl.CostEstimate(flops=1, bytes_accessed=1, transcendentals=0),
        name="toeplitz_conv",
    )(pieces, bias)


def partner(me, step, tp):
    chips, other = step
    return (me // CORES + chips) % (tp // CORES) * CORES + (me % CORES + other) % CORES


def source(me, step, tp):
    chips, other = step
    return (me // CORES + tp // CORES - chips) % (tp // CORES) * CORES + (me % CORES + CORES - other) % CORES


def exchanges(tp):
    steps = [(chips, other) for chips in range(tp // CORES) for other in range(CORES)][1:]
    early = (tp // CORES // 2, 0)
    return [early] + [step for step in reversed(steps) if step != early]


def prepare_kernel(key_ref, value_ref, taps_ref, w_ref, pieces_ref, *refs):
    shards, _, share, _ = pieces_ref.shape
    tp = lax.axis_size("tp")
    feats = w_ref.shape[1] // tp
    me = lax.axis_index("tp")
    plan = exchanges(tp)[: len(refs) - 5]
    cuts, (key, value, taps, in_sems, sems) = refs[: len(plan)], refs[len(plan) :]
    loads = []
    for place, (ref, held) in enumerate(((key_ref, key), (value_ref, value), (taps_ref, taps))):
        loads.append(pltpu.make_async_copy(ref, held, in_sems.at[place]))
        loads[-1].start()
    copies = []
    for place, step in enumerate(plan):
        column = pl.multiple_of(partner(me, step, tp) * feats, LANES)
        cut = w_ref.at[:, pl.ds(column, feats)]
        copies.append(pltpu.make_async_copy(cut, cuts[place], sems.at[place]))
        copies[-1].start()
    for load in loads:
        load.wait()
    for shard in range(shards):
        rows = pl.ds(shard * share, share)
        signal = key[rows, :].astype(jnp.float32) * value[rows, :].astype(jnp.float32)
        pieces_ref[shard, 0] = signal.astype(jnp.bfloat16)
        pieces_ref[shard, 1] = taps[rows, :].astype(jnp.bfloat16)
    for copy in copies:
        copy.wait()


def prepare(key_k, value_v, filter_taps, w_out, shards, tp):
    channels, seq_dev = key_k.shape
    feats = w_out.shape[1] // tp
    plan = exchanges(tp)[:1]
    vmem, hbm = pl.BlockSpec(memory_space=pltpu.VMEM), pl.BlockSpec(memory_space=pltpu.HBM)
    return pl.pallas_call(
        prepare_kernel,
        out_shape=[pltpu.VMEM((shards, 2, channels // shards, seq_dev), jnp.bfloat16)]
        + [pltpu.VMEM((channels, feats), jnp.bfloat16)] * len(plan),
        in_specs=[hbm, hbm, hbm, hbm],
        out_specs=[vmem] * (1 + len(plan)),
        scratch_shapes=[
            pltpu.VMEM(key_k.shape, key_k.dtype),
            pltpu.VMEM(value_v.shape, value_v.dtype),
            pltpu.VMEM(filter_taps.shape, filter_taps.dtype),
            pltpu.SemaphoreType.DMA((3,)),
            pltpu.SemaphoreType.DMA((len(plan),)),
        ],
        compiler_params=pltpu.CompilerParams(vmem_limit_bytes=8 * 2**20),
        cost_estimate=pl.CostEstimate(flops=channels * seq_dev, bytes_accessed=4 * w_out.size, transcendentals=0),
        name="prepare",
    )(*(pltpu.with_memory_space_constraint(x, pltpu.HBM) for x in (key_k, value_v, filter_taps, w_out)))


def gate_kernel(conv_ref, *refs):
    gates, out_ref = refs[:-1], refs[-1]
    blocks, chips, share, _ = conv_ref.shape
    channels = blocks * share
    row = lax.axis_index("tp") // CORES
    for step, gate_ref in enumerate(gates):
        other = (row + chips - step) % chips
        for block in range(blocks):
            rows = pl.ds(block * share, share)
            gated = gate_ref[rows, :].astype(jnp.float32) * conv_ref[block, other].astype(jnp.float32)
            out_ref[pl.ds(step * channels + block * share, share), :] = gated.astype(jnp.bfloat16)


def gate(convolved, gates):
    blocks, chips, share, seq_dev = convolved.shape
    return pl.pallas_call(
        gate_kernel,
        out_shape=pltpu.VMEM((chips * blocks * share, seq_dev), jnp.bfloat16),
        in_specs=[pl.BlockSpec(memory_space=pltpu.VMEM)] * (1 + chips),
        out_specs=pl.BlockSpec(memory_space=pltpu.VMEM),
        compiler_params=pltpu.CompilerParams(vmem_limit_bytes=8 * 2**20),
        name="gate",
    )(convolved, *(pltpu.with_memory_space_constraint(x, pltpu.VMEM) for x in gates))


def project_kernel(gated_ref, own_ref, *refs):
    weights, out_ref = (own_ref, *refs[:-1]), refs[-1]
    tp = lax.axis_size("tp")
    channels = own_ref.shape[0]
    core = lax.axis_index("tp") % CORES
    total = None
    for weight_ref, (chips, other) in zip(weights, [(0, 0)] + exchanges(tp)):
        place = (core + CORES - other) % CORES * (tp // CORES) + chips
        term = lax.dot_general(
            weight_ref[...],
            gated_ref[pl.ds(pl.multiple_of(place * channels, channels), channels), :],
            (((0,), (0,)), ((), ())),
            preferred_element_type=jnp.float32,
        )
        total = term if total is None else total + term
    out_ref[...] = total.astype(jnp.bfloat16)


def project(gathered, own, weights):
    channels, feats = own.shape
    rows, seq_dev = gathered.shape
    return pl.pallas_call(
        project_kernel,
        out_shape=jax.ShapeDtypeStruct((feats, seq_dev), jnp.bfloat16),
        in_specs=[pl.BlockSpec(memory_space=pltpu.VMEM)] * (2 + len(weights)),
        out_specs=pl.BlockSpec(memory_space=pltpu.VMEM),
        compiler_params=pltpu.CompilerParams(vmem_limit_bytes=24 * 2**20),
        cost_estimate=pl.CostEstimate(
            flops=2 * rows * feats * seq_dev, bytes_accessed=2 * rows * (feats + seq_dev), transcendentals=0
        ),
        name="project",
    )(gathered, own, *weights)


def body(gate_q, key_k, value_v, filter_taps, skip_bias, w_out):
    channels, seq_dev = key_k.shape
    shards = lax.axis_size("ctx")
    tp = lax.axis_size("tp")
    me = lax.axis_index("tp")
    chips = tp // CORES
    feats = w_out.shape[1] // tp

    def exchange(array, step):
        return lax.ppermute(array, "tp", [(i, partner(i, step, tp)) for i in range(tp)])

    pieces, *cuts = prepare(key_k, value_v, filter_taps, w_out, shards, tp)
    for step in exchanges(tp)[len(cuts) :]:
        cuts.append(lax.dynamic_slice_in_dim(w_out, partner(me, step, tp) * feats, feats, 1))
    weights = [exchange(cut, step) for cut, step in zip(cuts, exchanges(tp))]
    gates = [gate_q] + [exchange(gate_q, (step, 0)) for step in range(1, chips)]

    pieces = lax.all_to_all(pieces, "ctx", split_axis=0, concat_axis=0, tiled=True)
    convolved = convolve(pieces, skip_bias.reshape(channels, 1), chips)
    convolved, weights[0] = lax.optimization_barrier((convolved, weights[0]))
    convolved = lax.all_to_all(
        convolved.reshape(shards * chips, channels // shards, seq_dev),
        ("ctx", "tp"),
        split_axis=0,
        concat_axis=0,
        tiled=True,
        axis_index_groups=[
            [shard * tp + chip * CORES + core for shard in range(shards) for chip in range(chips)] for core in range(CORES)
        ],
    )
    own = lax.dynamic_slice_in_dim(w_out, me * feats, feats, 1)
    convolved, own, gates, weights = lax.optimization_barrier((convolved, own, gates, weights))
    gated_vals = gate(convolved.reshape(shards, chips, channels // shards, seq_dev), gates)
    gathered = lax.all_gather(
        gated_vals,
        "tp",
        axis=0,
        tiled=True,
        axis_index_groups=[[chip * CORES + core for core in range(CORES)] for chip in range(chips)],
    )
    return project(gathered, own, weights)


def solution(mesh):
    return jax.shard_map(
        body,
        mesh=mesh,
        in_specs=(P("tp", "ctx"), P("tp", "ctx"), P("tp", "ctx"), P("tp", "ctx"), P("tp"), P("tp", None)),
        out_specs=P("tp", "ctx"),
        check_vma=False,
    )
```

```python
import jax
import jax.numpy as jnp
from jax import lax
from jax.experimental import pallas as pl
from jax.experimental.pallas import tpu as pltpu
from jax.sharding import PartitionSpec as P

LANES = 128
PACK = 16
SUB = 16
PHASES = LANES // SUB
PARTS = 4
CORES = 2


def pitches(lines):
    pad = lines - PHASES
    return pad, (pad + lines) | 1, lines | 1


def conv_kernel(x_ref, bias_ref, y_ref, taps, rows, sums, result, sems):
    blocks, _, chans, seq_dev = x_ref.shape
    halves = seq_dev // LANES
    lines = blocks * halves
    length = lines * LANES
    pad, row_pitch, sum_pitch = pitches(lines)

    taps[:, pl.ds(0, LANES)] = jnp.zeros((chans, LANES), jnp.float32)
    for phase in range(PHASES):
        for chan in range(chans):
            rows[phase, pl.ds(chan * row_pitch, pad), :] = jnp.zeros((pad, LANES), jnp.float32)
    size = 8 if chans % 8 == 0 else chans
    lane = lax.broadcasted_iota(jnp.int32, (size, LANES), 1)
    bits = PHASES.bit_length() - 1
    odd = [lane // (SUB << bit) % 2 == 1 for bit in range(bits)]
    for begin in range(0, chans, size):
        history = [[[jnp.zeros((size, LANES), jnp.float32)] * PHASES] * (1 << bit) for bit in range(bits)]
        for line in range(lines):
            block, half = divmod(line, halves)
            fresh = x_ref[block, 0, pl.ds(begin, size), pl.ds(half * LANES, LANES)].astype(jnp.float32)
            level = [fresh] + [pltpu.roll(fresh, SUB * turn, axis=1) for turn in range(1, PHASES)]
            for bit in range(bits):
                step = 1 << bit
                past = history[bit][0]
                history[bit] = history[bit][1:] + [level]
                level = [jnp.where(odd[bit], past[(turn + step) % PHASES], level[turn]) for turn in range(PHASES)]
            for phase in range(PHASES):
                rows[phase, pl.ds(begin * row_pitch + pad + line, size, stride=row_pitch), :] = level[-phase % PHASES]
    for line in range(lines):
        block, half = divmod(line, halves)
        taps[:, pl.ds(LANES + line * LANES, LANES)] = x_ref[block, 1, :, pl.ds(half * LANES, LANES)].astype(jnp.float32)

    def channel(chan, _):
        wide = jnp.broadcast_to(taps[pl.ds(chan, 1), :], (PACK, LANES + length))
        skew = pltpu.roll(wide, 0, 1, stride=1, stride_axis=0).astype(jnp.bfloat16)
        toeplitz = jnp.concatenate([skew[:, (line + 1) * LANES : (line + 2) * LANES] for line in range(lines)], 0)
        base = chan * row_pitch + pad
        left = jnp.concatenate(
            [
                jnp.concatenate(
                    [
                        rows[phase, pl.ds(base - PHASES * step, lines), :].astype(jnp.bfloat16)
                        for step in range(lines // PHASES)
                    ],
                    1,
                )
                for phase in range(PHASES)
            ],
            0,
        )
        total = jnp.dot(left, toeplitz, preferred_element_type=jnp.float32)
        for phase in range(PHASES):
            sums[phase, pl.ds(chan * sum_pitch, lines), :] = total[phase * lines : (phase + 1) * lines]
        return 0

    lax.fori_loop(0, chans, channel, 0, unroll=True)

    first = pl.multiple_of(lax.axis_index("ctx") * chans, chans)
    size = PACK if chans % PACK == 0 else chans
    lane = lax.broadcasted_iota(jnp.int32, (size, LANES), 1)
    copies = []
    for begin in range(0, chans, size):
        part = pl.ds(begin, size)
        bias = jnp.broadcast_to(bias_ref[pl.ds(first + begin, size), :], (size, LANES))
        older = [jnp.zeros((size, LANES), jnp.float32)] * PHASES
        for line in range(lines):
            block, half = divmod(line, halves)
            cut = pl.ds(half * LANES, LANES)
            now = [sums[phase, pl.ds(begin * sum_pitch + line, size, stride=sum_pitch), :] for phase in range(PHASES)]
            value = now[0] + bias * x_ref[block, 0, part, cut].astype(jnp.float32)
            for phase in range(1, PHASES):
                mixed = jnp.where(lane < LANES - SUB * phase, now[phase], older[phase])
                value = value + pltpu.roll(mixed, SUB * phase, axis=1)
            older = now
            result[block, part, cut] = value.astype(jnp.bfloat16)
        for copy in range(y_ref.shape[1]):
            sem = sems.at[begin // size, copy]
            copies.append(pltpu.make_async_copy(result.at[:, part, :], y_ref.at[:, copy, part, :], sem))
            copies[-1].start()
    for copy in copies:
        copy.wait()


def convolve(pieces, bias, copies):
    blocks, _, chans, seq_dev = pieces.shape
    lines = blocks * seq_dev // LANES
    _, row_pitch, sum_pitch = pitches(lines)
    return pl.pallas_call(
        conv_kernel,
        out_shape=jax.ShapeDtypeStruct((blocks, copies, chans, seq_dev), jnp.bfloat16),
        in_specs=[pl.BlockSpec(memory_space=pltpu.VMEM)] * 2,
        out_specs=pl.BlockSpec(memory_space=pltpu.HBM),
        scratch_shapes=[
            pltpu.VMEM((chans, LANES + lines * LANES), jnp.float32),
            pltpu.VMEM((PHASES, chans * row_pitch, LANES), jnp.float32),
            pltpu.VMEM((PHASES, chans * sum_pitch, LANES), jnp.float32),
            pltpu.VMEM((blocks, chans, seq_dev), jnp.bfloat16),
            pltpu.SemaphoreType.DMA((pl.cdiv(chans, PACK), copies)),
        ],
        compiler_params=pltpu.CompilerParams(vmem_limit_bytes=16 * 2**20),
        cost_estimate=pl.CostEstimate(flops=1, bytes_accessed=1, transcendentals=0),
        name="toeplitz_conv",
    )(pieces, bias)


def partner(me, step, tp):
    chips, other = step
    return (me // CORES + chips) % (tp // CORES) * CORES + (me % CORES + other) % CORES


def source(me, step, tp):
    chips, other = step
    return (me // CORES + tp // CORES - chips) % (tp // CORES) * CORES + (me % CORES + CORES - other) % CORES


def exchanges(tp):
    steps = [(chips, other) for chips in range(tp // CORES) for other in range(CORES)][1:]
    early = (tp // CORES // 2, 0)
    return [early] + [step for step in reversed(steps) if step != early]


def prepare_kernel(key_ref, value_ref, taps_ref, w_ref, pieces_ref, *refs):
    shards, _, share, _ = pieces_ref.shape
    tp = lax.axis_size("tp")
    feats = w_ref.shape[1] // tp
    me = lax.axis_index("tp")
    plan = exchanges(tp)[: len(refs) - 5]
    cuts, (key, value, taps, in_sems, sems) = refs[: len(plan)], refs[len(plan) :]
    loads = []
    for place, (ref, held) in enumerate(((key_ref, key), (value_ref, value), (taps_ref, taps))):
        loads.append(pltpu.make_async_copy(ref, held, in_sems.at[place]))
        loads[-1].start()
    copies = []
    for place, step in enumerate(plan):
        column = pl.multiple_of(partner(me, step, tp) * feats, LANES)
        cut = w_ref.at[:, pl.ds(column, feats)]
        copies.append(pltpu.make_async_copy(cut, cuts[place], sems.at[place]))
        copies[-1].start()
    for load in loads:
        load.wait()
    for shard in range(shards):
        rows = pl.ds(shard * share, share)
        signal = key[rows, :].astype(jnp.float32) * value[rows, :].astype(jnp.float32)
        pieces_ref[shard, 0] = signal.astype(jnp.bfloat16)
        pieces_ref[shard, 1] = taps[rows, :].astype(jnp.bfloat16)
    for copy in copies:
        copy.wait()


def prepare(key_k, value_v, filter_taps, w_out, shards, tp):
    channels, seq_dev = key_k.shape
    feats = w_out.shape[1] // tp
    plan = exchanges(tp)[:1]
    vmem, hbm = pl.BlockSpec(memory_space=pltpu.VMEM), pl.BlockSpec(memory_space=pltpu.HBM)
    return pl.pallas_call(
        prepare_kernel,
        out_shape=[pltpu.VMEM((shards, 2, channels // shards, seq_dev), jnp.bfloat16)]
        + [pltpu.VMEM((channels, feats), jnp.bfloat16)] * len(plan),
        in_specs=[hbm, hbm, hbm, hbm],
        out_specs=[vmem] * (1 + len(plan)),
        scratch_shapes=[
            pltpu.VMEM(key_k.shape, key_k.dtype),
            pltpu.VMEM(value_v.shape, value_v.dtype),
            pltpu.VMEM(filter_taps.shape, filter_taps.dtype),
            pltpu.SemaphoreType.DMA((3,)),
            pltpu.SemaphoreType.DMA((len(plan),)),
        ],
        compiler_params=pltpu.CompilerParams(vmem_limit_bytes=8 * 2**20),
        cost_estimate=pl.CostEstimate(flops=channels * seq_dev, bytes_accessed=4 * w_out.size, transcendentals=0),
        name="prepare",
    )(*(pltpu.with_memory_space_constraint(x, pltpu.HBM) for x in (key_k, value_v, filter_taps, w_out)))


def gate_kernel(conv_ref, *refs):
    gates, out_ref = refs[:-1], refs[-1]
    blocks, chips, share, _ = conv_ref.shape
    channels = blocks * share
    row = lax.axis_index("tp") // CORES
    for step, gate_ref in enumerate(gates):
        other = (row + chips - step) % chips
        for block in range(blocks):
            rows = pl.ds(block * share, share)
            gated = gate_ref[rows, :].astype(jnp.float32) * conv_ref[block, other].astype(jnp.float32)
            out_ref[pl.ds(step * channels + block * share, share), :] = gated.astype(jnp.bfloat16)


def gate(convolved, gates):
    blocks, chips, share, seq_dev = convolved.shape
    return pl.pallas_call(
        gate_kernel,
        out_shape=pltpu.VMEM((chips * blocks * share, seq_dev), jnp.bfloat16),
        in_specs=[pl.BlockSpec(memory_space=pltpu.VMEM)] * (1 + chips),
        out_specs=pl.BlockSpec(memory_space=pltpu.VMEM),
        compiler_params=pltpu.CompilerParams(vmem_limit_bytes=8 * 2**20),
        name="gate",
    )(convolved, *(pltpu.with_memory_space_constraint(x, pltpu.VMEM) for x in gates))


def project_own_kernel(gated_ref, *refs):
    *weights, sum_ref, turned_ref = refs
    mine, others = weights[: len(weights) // CORES], weights[len(weights) // CORES :]
    channels = weights[0].shape[0]
    total = None
    for place, weight_ref in enumerate(mine):
        term = lax.dot_general(
            weight_ref[...],
            gated_ref[pl.ds(place * channels, channels), :],
            (((0,), (0,)), ((), ())),
            preferred_element_type=jnp.float32,
        )
        total = term if total is None else total + term
    sum_ref[...] = total
    for place, weight_ref in enumerate(others):
        turned_ref[:, pl.ds(place * channels, channels)] = weight_ref[...].T


def project_other_kernel(gated_ref, sum_ref, turned_ref, out_ref, held, sems):
    parts = sems.shape[0]
    count = out_ref.shape[0] // parts
    copies = []
    for part in range(parts):
        rows = pl.ds(part * count, count)
        term = jnp.dot(turned_ref[rows, :], gated_ref[...], preferred_element_type=jnp.float32)
        held[rows, :] = (sum_ref[rows, :] + term).astype(jnp.bfloat16)
        copies.append(pltpu.make_async_copy(held.at[rows, :], out_ref.at[rows, :], sems.at[part]))
        copies[-1].start()
    for copy in copies:
        copy.wait()


def project(gated_vals, others, weights):
    channels, feats = weights[0].shape
    rows, seq_dev = gated_vals.shape
    vmem = pl.BlockSpec(memory_space=pltpu.VMEM)
    cost = pl.CostEstimate(
        flops=2 * rows * feats * seq_dev, bytes_accessed=2 * rows * (feats + seq_dev), transcendentals=0
    )
    so_far, turned = pl.pallas_call(
        project_own_kernel,
        out_shape=[
            jax.ShapeDtypeStruct((feats, seq_dev), jnp.float32),
            jax.ShapeDtypeStruct((feats, rows), jnp.bfloat16),
        ],
        in_specs=[vmem] * (1 + len(weights)),
        out_specs=[vmem] * 2,
        compiler_params=pltpu.CompilerParams(vmem_limit_bytes=16 * 2**20),
        cost_estimate=cost,
        name="project_own",
    )(gated_vals, *weights)
    return pl.pallas_call(
        project_other_kernel,
        out_shape=jax.ShapeDtypeStruct((feats, seq_dev), jnp.bfloat16),
        in_specs=[vmem] * 3,
        out_specs=pl.BlockSpec(memory_space=pltpu.HBM),
        scratch_shapes=[pltpu.VMEM((feats, seq_dev), jnp.bfloat16), pltpu.SemaphoreType.DMA((PARTS,))],
        compiler_params=pltpu.CompilerParams(vmem_limit_bytes=16 * 2**20),
        cost_estimate=cost,
        name="project_other",
    )(others, so_far, turned)


def body(gate_q, key_k, value_v, filter_taps, skip_bias, w_out):
    channels, seq_dev = key_k.shape
    shards = lax.axis_size("ctx")
    tp = lax.axis_size("tp")
    me = lax.axis_index("tp")
    chips = tp // CORES
    feats = w_out.shape[1] // tp

    def exchange(array, step):
        return lax.ppermute(array, "tp", [(i, partner(i, step, tp)) for i in range(tp)])

    pieces, *cuts = prepare(key_k, value_v, filter_taps, w_out, shards, tp)
    for step in exchanges(tp)[len(cuts) :]:
        cuts.append(lax.dynamic_slice_in_dim(w_out, partner(me, step, tp) * feats, feats, 1))
    weights = [exchange(cut, step) for cut, step in zip(cuts, exchanges(tp))]
    gates = [gate_q] + [exchange(gate_q, (step, 0)) for step in range(1, chips)]

    pieces = lax.all_to_all(pieces, "ctx", split_axis=0, concat_axis=0, tiled=True)
    convolved = convolve(pieces, skip_bias.reshape(channels, 1), chips)
    convolved, weights[0] = lax.optimization_barrier((convolved, weights[0]))
    convolved = lax.all_to_all(
        convolved.reshape(shards * chips, channels // shards, seq_dev),
        ("ctx", "tp"),
        split_axis=0,
        concat_axis=0,
        tiled=True,
        axis_index_groups=[
            [shard * tp + chip * CORES + core for shard in range(shards) for chip in range(chips)] for core in range(CORES)
        ],
    )
    own = lax.dynamic_slice_in_dim(w_out, me * feats, feats, 1)
    convolved, own, gates, weights = lax.optimization_barrier((convolved, own, gates, weights))
    gated_vals = gate(convolved.reshape(shards, chips, channels // shards, seq_dev), gates)
    others = exchange(gated_vals, (0, 1))
    blocks = dict(zip([(0, 0)] + exchanges(tp), [own, *weights]))
    ordered = [blocks[chip, core] for core in range(CORES) for chip in range(chips)]
    return project(gated_vals, others, ordered)


def solution(mesh):
    return jax.shard_map(
        body,
        mesh=mesh,
        in_specs=(P("tp", "ctx"), P("tp", "ctx"), P("tp", "ctx"), P("tp", "ctx"), P("tp"), P("tp", None)),
        out_specs=P("tp", "ctx"),
        check_vma=False,
    )
```

```python
import jax
import jax.numpy as jnp
from jax import lax
from jax.experimental import pallas as pl
from jax.experimental.pallas import tpu as pltpu
from jax.sharding import PartitionSpec as P

LANES = 128
PACK = 16
SUB = 16
PHASES = LANES // SUB
PARTS = 4
CORES = 2


def ctx_order(shards):
    middle = shards // 2
    return [middle] + [shard for shard in range(shards) if shard != middle]


def pitches(lines):
    pad = lines - PHASES
    return pad, (pad + lines) | 1, lines | 1


def conv_kernel(x_ref, bias_ref, y_ref, taps, rows, sums, result, sems):
    blocks, _, chans, seq_dev = x_ref.shape
    halves = seq_dev // LANES
    place = ctx_order(blocks).index
    lines = blocks * halves
    length = lines * LANES
    pad, row_pitch, sum_pitch = pitches(lines)

    taps[:, pl.ds(0, LANES)] = jnp.zeros((chans, LANES), jnp.float32)
    for phase in range(PHASES):
        for chan in range(chans):
            rows[phase, pl.ds(chan * row_pitch, pad), :] = jnp.zeros((pad, LANES), jnp.float32)
    size = 8 if chans % 8 == 0 else chans
    lane = lax.broadcasted_iota(jnp.int32, (size, LANES), 1)
    bits = PHASES.bit_length() - 1
    odd = [lane // (SUB << bit) % 2 == 1 for bit in range(bits)]
    for begin in range(0, chans, size):
        history = [[[jnp.zeros((size, LANES), jnp.float32)] * PHASES] * (1 << bit) for bit in range(bits)]
        for line in range(lines):
            block, half = divmod(line, halves)
            fresh = x_ref[place(block), 0, pl.ds(begin, size), pl.ds(half * LANES, LANES)].astype(jnp.float32)
            level = [fresh] + [pltpu.roll(fresh, SUB * turn, axis=1) for turn in range(1, PHASES)]
            for bit in range(bits):
                step = 1 << bit
                past = history[bit][0]
                history[bit] = history[bit][1:] + [level]
                level = [jnp.where(odd[bit], past[(turn + step) % PHASES], level[turn]) for turn in range(PHASES)]
            for phase in range(PHASES):
                rows[phase, pl.ds(begin * row_pitch + pad + line, size, stride=row_pitch), :] = level[-phase % PHASES]
    for line in range(lines):
        block, half = divmod(line, halves)
        taps[:, pl.ds(LANES + line * LANES, LANES)] = x_ref[place(block), 1, :, pl.ds(half * LANES, LANES)].astype(jnp.float32)

    def channel(chan, _):
        wide = jnp.broadcast_to(taps[pl.ds(chan, 1), :], (PACK, LANES + length))
        skew = pltpu.roll(wide, 0, 1, stride=1, stride_axis=0).astype(jnp.bfloat16)
        toeplitz = jnp.concatenate([skew[:, (line + 1) * LANES : (line + 2) * LANES] for line in range(lines)], 0)
        base = chan * row_pitch + pad
        left = jnp.concatenate(
            [
                jnp.concatenate(
                    [
                        rows[phase, pl.ds(base - PHASES * step, lines), :].astype(jnp.bfloat16)
                        for step in range(lines // PHASES)
                    ],
                    1,
                )
                for phase in range(PHASES)
            ],
            0,
        )
        total = jnp.dot(left, toeplitz, preferred_element_type=jnp.float32)
        for phase in range(PHASES):
            sums[phase, pl.ds(chan * sum_pitch, lines), :] = total[phase * lines : (phase + 1) * lines]
        return 0

    lax.fori_loop(0, chans, channel, 0, unroll=True)

    first = pl.multiple_of(lax.axis_index("ctx") * chans, chans)
    size = PACK if chans % PACK == 0 else chans
    lane = lax.broadcasted_iota(jnp.int32, (size, LANES), 1)
    copies = []
    for begin in range(0, chans, size):
        part = pl.ds(begin, size)
        bias = jnp.broadcast_to(bias_ref[pl.ds(first + begin, size), :], (size, LANES))
        older = [jnp.zeros((size, LANES), jnp.float32)] * PHASES
        for line in range(lines):
            block, half = divmod(line, halves)
            cut = pl.ds(half * LANES, LANES)
            now = [sums[phase, pl.ds(begin * sum_pitch + line, size, stride=sum_pitch), :] for phase in range(PHASES)]
            value = now[0] + bias * x_ref[place(block), 0, part, cut].astype(jnp.float32)
            for phase in range(1, PHASES):
                mixed = jnp.where(lane < LANES - SUB * phase, now[phase], older[phase])
                value = value + pltpu.roll(mixed, SUB * phase, axis=1)
            older = now
            result[place(block), part, cut] = value.astype(jnp.bfloat16)
        for copy in range(y_ref.shape[1]):
            sem = sems.at[begin // size, copy]
            copies.append(pltpu.make_async_copy(result.at[:, part, :], y_ref.at[:, copy, part, :], sem))
            copies[-1].start()
    for copy in copies:
        copy.wait()


def convolve(pieces, bias, copies):
    blocks, _, chans, seq_dev = pieces.shape
    lines = blocks * seq_dev // LANES
    _, row_pitch, sum_pitch = pitches(lines)
    return pl.pallas_call(
        conv_kernel,
        out_shape=jax.ShapeDtypeStruct((blocks, copies, chans, seq_dev), jnp.bfloat16),
        in_specs=[pl.BlockSpec(memory_space=pltpu.VMEM)] * 2,
        out_specs=pl.BlockSpec(memory_space=pltpu.HBM),
        scratch_shapes=[
            pltpu.VMEM((chans, LANES + lines * LANES), jnp.float32),
            pltpu.VMEM((PHASES, chans * row_pitch, LANES), jnp.float32),
            pltpu.VMEM((PHASES, chans * sum_pitch, LANES), jnp.float32),
            pltpu.VMEM((blocks, chans, seq_dev), jnp.bfloat16),
            pltpu.SemaphoreType.DMA((pl.cdiv(chans, PACK), copies)),
        ],
        compiler_params=pltpu.CompilerParams(vmem_limit_bytes=16 * 2**20),
        cost_estimate=pl.CostEstimate(flops=1, bytes_accessed=1, transcendentals=0),
        name="toeplitz_conv",
    )(pieces, bias)


def partner(me, step, tp):
    chips, other = step
    return (me // CORES + chips) % (tp // CORES) * CORES + (me % CORES + other) % CORES


def source(me, step, tp):
    chips, other = step
    return (me // CORES + tp // CORES - chips) % (tp // CORES) * CORES + (me % CORES + CORES - other) % CORES


def exchanges(tp):
    steps = [(chips, other) for chips in range(tp // CORES) for other in range(CORES)][1:]
    early = (tp // CORES // 2, 0)
    return [early] + [step for step in reversed(steps) if step != early]


def prepare_kernel(key_ref, value_ref, taps_ref, w_ref, pieces_ref, *refs):
    shards, _, share, _ = pieces_ref.shape
    tp = lax.axis_size("tp")
    feats = w_ref.shape[1] // tp
    me = lax.axis_index("tp")
    plan = exchanges(tp)[: len(refs) - 5]
    cuts, (key, value, taps, in_sems, sems) = refs[: len(plan)], refs[len(plan) :]
    loads = []
    for place, (ref, held) in enumerate(((key_ref, key), (value_ref, value), (taps_ref, taps))):
        loads.append(pltpu.make_async_copy(ref, held, in_sems.at[place]))
        loads[-1].start()
    copies = []
    for place, step in enumerate(plan):
        column = pl.multiple_of(partner(me, step, tp) * feats, LANES)
        cut = w_ref.at[:, pl.ds(column, feats)]
        copies.append(pltpu.make_async_copy(cut, cuts[place], sems.at[place]))
        copies[-1].start()
    for load in loads:
        load.wait()
    for place, shard in enumerate(ctx_order(shards)):
        rows = pl.ds(shard * share, share)
        signal = key[rows, :].astype(jnp.float32) * value[rows, :].astype(jnp.float32)
        pieces_ref[place, 0] = signal.astype(jnp.bfloat16)
        pieces_ref[place, 1] = taps[rows, :].astype(jnp.bfloat16)
    for copy in copies:
        copy.wait()


def prepare(key_k, value_v, filter_taps, w_out, shards, tp):
    channels, seq_dev = key_k.shape
    feats = w_out.shape[1] // tp
    plan = exchanges(tp)[:1]
    vmem, hbm = pl.BlockSpec(memory_space=pltpu.VMEM), pl.BlockSpec(memory_space=pltpu.HBM)
    return pl.pallas_call(
        prepare_kernel,
        out_shape=[pltpu.VMEM((shards, 2, channels // shards, seq_dev), jnp.bfloat16)]
        + [pltpu.VMEM((channels, feats), jnp.bfloat16)] * len(plan),
        in_specs=[hbm, hbm, hbm, hbm],
        out_specs=[vmem] * (1 + len(plan)),
        scratch_shapes=[
            pltpu.VMEM(key_k.shape, key_k.dtype),
            pltpu.VMEM(value_v.shape, value_v.dtype),
            pltpu.VMEM(filter_taps.shape, filter_taps.dtype),
            pltpu.SemaphoreType.DMA((3,)),
            pltpu.SemaphoreType.DMA((len(plan),)),
        ],
        compiler_params=pltpu.CompilerParams(vmem_limit_bytes=8 * 2**20),
        cost_estimate=pl.CostEstimate(flops=channels * seq_dev, bytes_accessed=4 * w_out.size, transcendentals=0),
        name="prepare",
    )(*(pltpu.with_memory_space_constraint(x, pltpu.HBM) for x in (key_k, value_v, filter_taps, w_out)))


def gate_kernel(conv_ref, *refs):
    gates, out_ref = refs[:-1], refs[-1]
    blocks, chips, share, _ = conv_ref.shape
    channels = blocks * share
    row = lax.axis_index("tp") // CORES
    for step, gate_ref in enumerate(gates):
        other = (row + chips - step) % chips
        for place, block in enumerate(ctx_order(blocks)):
            rows = pl.ds(block * share, share)
            gated = gate_ref[rows, :].astype(jnp.float32) * conv_ref[place, chips - 1 - other].astype(jnp.float32)
            out_ref[pl.ds(step * channels + block * share, share), :] = gated.astype(jnp.bfloat16)


def gate(convolved, gates):
    blocks, chips, share, seq_dev = convolved.shape
    return pl.pallas_call(
        gate_kernel,
        out_shape=pltpu.VMEM((chips * blocks * share, seq_dev), jnp.bfloat16),
        in_specs=[pl.BlockSpec(memory_space=pltpu.VMEM)] * (1 + chips),
        out_specs=pl.BlockSpec(memory_space=pltpu.VMEM),
        compiler_params=pltpu.CompilerParams(vmem_limit_bytes=8 * 2**20),
        name="gate",
    )(convolved, *(pltpu.with_memory_space_constraint(x, pltpu.VMEM) for x in gates))


def project_own_kernel(gated_ref, *refs):
    *weights, sum_ref, turned_ref = refs
    mine, others = weights[: len(weights) // CORES], weights[len(weights) // CORES :]
    channels = weights[0].shape[0]
    total = None
    for place, weight_ref in enumerate(mine):
        term = lax.dot_general(
            weight_ref[...],
            gated_ref[pl.ds(place * channels, channels), :],
            (((0,), (0,)), ((), ())),
            preferred_element_type=jnp.float32,
        )
        total = term if total is None else total + term
    sum_ref[...] = total
    for place, weight_ref in enumerate(others):
        turned_ref[:, pl.ds(place * channels, channels)] = weight_ref[...].T


def project_other_kernel(gated_ref, sum_ref, turned_ref, out_ref, held, sems):
    parts = sems.shape[0]
    count = out_ref.shape[0] // parts
    copies = []
    for part in range(parts):
        rows = pl.ds(part * count, count)
        term = jnp.dot(turned_ref[rows, :], gated_ref[...], preferred_element_type=jnp.float32)
        held[rows, :] = (sum_ref[rows, :] + term).astype(jnp.bfloat16)
        copies.append(pltpu.make_async_copy(held.at[rows, :], out_ref.at[rows, :], sems.at[part]))
        copies[-1].start()
    for copy in copies:
        copy.wait()


def project(gated_vals, others, weights):
    channels, feats = weights[0].shape
    rows, seq_dev = gated_vals.shape
    vmem = pl.BlockSpec(memory_space=pltpu.VMEM)
    cost = pl.CostEstimate(
        flops=2 * rows * feats * seq_dev, bytes_accessed=2 * rows * (feats + seq_dev), transcendentals=0
    )
    so_far, turned = pl.pallas_call(
        project_own_kernel,
        out_shape=[
            jax.ShapeDtypeStruct((feats, seq_dev), jnp.float32),
            jax.ShapeDtypeStruct((feats, rows), jnp.bfloat16),
        ],
        in_specs=[vmem] * (1 + len(weights)),
        out_specs=[vmem] * 2,
        compiler_params=pltpu.CompilerParams(vmem_limit_bytes=16 * 2**20),
        cost_estimate=cost,
        name="project_own",
    )(gated_vals, *weights)
    return pl.pallas_call(
        project_other_kernel,
        out_shape=jax.ShapeDtypeStruct((feats, seq_dev), jnp.bfloat16),
        in_specs=[vmem] * 3,
        out_specs=pl.BlockSpec(memory_space=pltpu.HBM),
        scratch_shapes=[pltpu.VMEM((feats, seq_dev), jnp.bfloat16), pltpu.SemaphoreType.DMA((PARTS,))],
        compiler_params=pltpu.CompilerParams(vmem_limit_bytes=16 * 2**20),
        cost_estimate=cost,
        name="project_other",
    )(others, so_far, turned)


def body(gate_q, key_k, value_v, filter_taps, skip_bias, w_out):
    channels, seq_dev = key_k.shape
    shards = lax.axis_size("ctx")
    tp = lax.axis_size("tp")
    me = lax.axis_index("tp")
    chips = tp // CORES
    feats = w_out.shape[1] // tp

    def exchange(array, step):
        return lax.ppermute(array, "tp", [(i, partner(i, step, tp)) for i in range(tp)])

    pieces, *cuts = prepare(key_k, value_v, filter_taps, w_out, shards, tp)
    for step in exchanges(tp)[len(cuts) :]:
        cuts.append(lax.dynamic_slice_in_dim(w_out, partner(me, step, tp) * feats, feats, 1))
    weights = [exchange(cut, step) for cut, step in zip(cuts, exchanges(tp))]
    gates = [gate_q] + [exchange(gate_q, (step, 0)) for step in range(1, chips)]

    order = ctx_order(shards)
    pieces = lax.all_to_all(pieces, "ctx", split_axis=0, concat_axis=0, tiled=True, axis_index_groups=[order])
    convolved = convolve(pieces, skip_bias.reshape(channels, 1), chips)
    convolved, weights[0] = lax.optimization_barrier((convolved, weights[0]))
    convolved = lax.all_to_all(
        convolved.reshape(shards * chips, channels // shards, seq_dev),
        ("ctx", "tp"),
        split_axis=0,
        concat_axis=0,
        tiled=True,
        axis_index_groups=[
            [shard * tp + chip * CORES + core for shard in order for chip in reversed(range(chips))] for core in range(CORES)
        ],
    )
    own = lax.dynamic_slice_in_dim(w_out, me * feats, feats, 1)
    convolved, own, gates, weights = lax.optimization_barrier((convolved, own, gates, weights))
    gated_vals = gate(convolved.reshape(shards, chips, channels // shards, seq_dev), gates)
    others = exchange(gated_vals, (0, 1))
    blocks = dict(zip([(0, 0)] + exchanges(tp), [own, *weights]))
    ordered = [blocks[chip, core] for core in range(CORES) for chip in range(chips)]
    return project(gated_vals, others, ordered)


def solution(mesh):
    return jax.shard_map(
        body,
        mesh=mesh,
        in_specs=(P("tp", "ctx"), P("tp", "ctx"), P("tp", "ctx"), P("tp", "ctx"), P("tp"), P("tp", None)),
        out_specs=P("tp", "ctx"),
        check_vma=False,
    )
```

```python
import jax
import jax.numpy as jnp
from jax import lax
from jax.experimental import pallas as pl
from jax.experimental.pallas import tpu as pltpu
from jax.sharding import PartitionSpec as P

LANES = 128
PACK = 16
SUB = 16
PHASES = LANES // SUB
PARTS = 4
CORES = 2


def ctx_order(shards):
    middle = shards // 2
    return [middle] + [shard for shard in range(shards) if shard != middle]


def pitches(lines):
    pad = lines - PHASES
    return pad, (pad + lines) | 1, lines | 1


def conv_kernel(x_ref, bias_ref, y_ref, taps, rows, sums, result, sems):
    blocks, _, chans, seq_dev = x_ref.shape
    halves = seq_dev // LANES
    place = ctx_order(blocks).index
    lines = blocks * halves
    length = lines * LANES
    pad, row_pitch, sum_pitch = pitches(lines)

    taps[:, pl.ds(0, LANES)] = jnp.zeros((chans, LANES), jnp.float32)
    for phase in range(PHASES):
        for chan in range(chans):
            rows[phase, pl.ds(chan * row_pitch, pad), :] = jnp.zeros((pad, LANES), jnp.float32)
    size = 8 if chans % 8 == 0 else chans
    lane = lax.broadcasted_iota(jnp.int32, (size, LANES), 1)
    bits = PHASES.bit_length() - 1
    odd = [lane // (SUB << bit) % 2 == 1 for bit in range(bits)]
    for begin in range(0, chans, size):
        history = [[[jnp.zeros((size, LANES), jnp.float32)] * PHASES] * (1 << bit) for bit in range(bits)]
        for line in range(lines):
            block, half = divmod(line, halves)
            fresh = x_ref[place(block), 0, pl.ds(begin, size), pl.ds(half * LANES, LANES)].astype(jnp.float32)
            level = [fresh] + [pltpu.roll(fresh, SUB * turn, axis=1) for turn in range(1, PHASES)]
            for bit in range(bits):
                step = 1 << bit
                past = history[bit][0]
                history[bit] = history[bit][1:] + [level]
                level = [jnp.where(odd[bit], past[(turn + step) % PHASES], level[turn]) for turn in range(PHASES)]
            for phase in range(PHASES):
                rows[phase, pl.ds(begin * row_pitch + pad + line, size, stride=row_pitch), :] = level[-phase % PHASES]
    for line in range(lines):
        block, half = divmod(line, halves)
        taps[:, pl.ds(LANES + line * LANES, LANES)] = x_ref[place(block), 1, :, pl.ds(half * LANES, LANES)].astype(jnp.float32)

    def channel(chan, _):
        wide = jnp.broadcast_to(taps[pl.ds(chan, 1), :], (PACK, LANES + length))
        skew = pltpu.roll(wide, 0, 1, stride=1, stride_axis=0).astype(jnp.bfloat16)
        toeplitz = jnp.concatenate([skew[:, (line + 1) * LANES : (line + 2) * LANES] for line in range(lines)], 0)
        base = chan * row_pitch + pad
        left = jnp.concatenate(
            [
                jnp.concatenate(
                    [
                        rows[phase, pl.ds(base - PHASES * step, lines), :].astype(jnp.bfloat16)
                        for step in range(lines // PHASES)
                    ],
                    1,
                )
                for phase in range(PHASES)
            ],
            0,
        )
        total = jnp.dot(left, toeplitz, preferred_element_type=jnp.float32)
        for phase in range(PHASES):
            sums[phase, pl.ds(chan * sum_pitch, lines), :] = total[phase * lines : (phase + 1) * lines]
        return 0

    lax.fori_loop(0, chans, channel, 0, unroll=True)

    first = pl.multiple_of(lax.axis_index("ctx") * chans, chans)
    size = PACK if chans % PACK == 0 else chans
    lane = lax.broadcasted_iota(jnp.int32, (size, LANES), 1)
    copies = []
    for begin in range(0, chans, size):
        part = pl.ds(begin, size)
        bias = jnp.broadcast_to(bias_ref[pl.ds(first + begin, size), :], (size, LANES))
        older = [jnp.zeros((size, LANES), jnp.float32)] * PHASES
        for line in range(lines):
            block, half = divmod(line, halves)
            cut = pl.ds(half * LANES, LANES)
            now = [sums[phase, pl.ds(begin * sum_pitch + line, size, stride=sum_pitch), :] for phase in range(PHASES)]
            value = now[0] + bias * x_ref[place(block), 0, part, cut].astype(jnp.float32)
            for phase in range(1, PHASES):
                mixed = jnp.where(lane < LANES - SUB * phase, now[phase], older[phase])
                value = value + pltpu.roll(mixed, SUB * phase, axis=1)
            older = now
            result[place(block), part, cut] = value.astype(jnp.bfloat16)
        for copy in range(y_ref.shape[1]):
            sem = sems.at[begin // size, copy]
            copies.append(pltpu.make_async_copy(result.at[:, part, :], y_ref.at[:, copy, part, :], sem))
            copies[-1].start()
    for copy in copies:
        copy.wait()


def convolve(pieces, bias, copies):
    blocks, _, chans, seq_dev = pieces.shape
    lines = blocks * seq_dev // LANES
    _, row_pitch, sum_pitch = pitches(lines)
    return pl.pallas_call(
        conv_kernel,
        out_shape=jax.ShapeDtypeStruct((blocks, copies, chans, seq_dev), jnp.bfloat16),
        in_specs=[pl.BlockSpec(memory_space=pltpu.VMEM)] * 2,
        out_specs=pl.BlockSpec(memory_space=pltpu.HBM),
        scratch_shapes=[
            pltpu.VMEM((chans, LANES + lines * LANES), jnp.float32),
            pltpu.VMEM((PHASES, chans * row_pitch, LANES), jnp.float32),
            pltpu.VMEM((PHASES, chans * sum_pitch, LANES), jnp.float32),
            pltpu.VMEM((blocks, chans, seq_dev), jnp.bfloat16),
            pltpu.SemaphoreType.DMA((pl.cdiv(chans, PACK), copies)),
        ],
        compiler_params=pltpu.CompilerParams(vmem_limit_bytes=16 * 2**20),
        cost_estimate=pl.CostEstimate(flops=1, bytes_accessed=1, transcendentals=0),
        name="toeplitz_conv",
    )(pieces, bias)


def partner(me, step, tp):
    chips, other = step
    return (me // CORES + chips) % (tp // CORES) * CORES + (me % CORES + other) % CORES


def source(me, step, tp):
    chips, other = step
    return (me // CORES + tp // CORES - chips) % (tp // CORES) * CORES + (me % CORES + CORES - other) % CORES


def exchanges(tp):
    steps = [(chips, other) for chips in range(tp // CORES) for other in range(CORES)][1:]
    early = (tp // CORES // 2, 0)
    return [early] + [step for step in reversed(steps) if step != early]


def prepare_kernel(key_ref, value_ref, taps_ref, w_ref, pieces_ref, *refs):
    shards, _, share, _ = pieces_ref.shape
    tp = lax.axis_size("tp")
    feats = w_ref.shape[1] // tp
    me = lax.axis_index("tp")
    plan = exchanges(tp)[: len(refs) - 5]
    cuts, (key, value, taps, in_sems, sems) = refs[: len(plan)], refs[len(plan) :]
    loads = []
    for place, (ref, held) in enumerate(((key_ref, key), (value_ref, value), (taps_ref, taps))):
        loads.append(pltpu.make_async_copy(ref, held, in_sems.at[place]))
        loads[-1].start()
    copies = []
    for place, step in enumerate(plan):
        column = pl.multiple_of(partner(me, step, tp) * feats, LANES)
        cut = w_ref.at[:, pl.ds(column, feats)]
        copies.append(pltpu.make_async_copy(cut, cuts[place], sems.at[place]))
        copies[-1].start()
    for load in loads:
        load.wait()
    for place, shard in enumerate(ctx_order(shards)):
        rows = pl.ds(shard * share, share)
        signal = key[rows, :].astype(jnp.float32) * value[rows, :].astype(jnp.float32)
        pieces_ref[place, 0] = signal.astype(jnp.bfloat16)
        pieces_ref[place, 1] = taps[rows, :].astype(jnp.bfloat16)
    for copy in copies:
        copy.wait()


def prepare(key_k, value_v, filter_taps, w_out, shards, tp):
    channels, seq_dev = key_k.shape
    feats = w_out.shape[1] // tp
    plan = exchanges(tp)[:1]
    vmem, hbm = pl.BlockSpec(memory_space=pltpu.VMEM), pl.BlockSpec(memory_space=pltpu.HBM)
    return pl.pallas_call(
        prepare_kernel,
        out_shape=[pltpu.VMEM((shards, 2, channels // shards, seq_dev), jnp.bfloat16)]
        + [pltpu.VMEM((channels, feats), jnp.bfloat16)] * len(plan),
        in_specs=[hbm, hbm, hbm, hbm],
        out_specs=[vmem] * (1 + len(plan)),
        scratch_shapes=[
            pltpu.VMEM(key_k.shape, key_k.dtype),
            pltpu.VMEM(value_v.shape, value_v.dtype),
            pltpu.VMEM(filter_taps.shape, filter_taps.dtype),
            pltpu.SemaphoreType.DMA((3,)),
            pltpu.SemaphoreType.DMA((len(plan),)),
        ],
        compiler_params=pltpu.CompilerParams(vmem_limit_bytes=8 * 2**20),
        cost_estimate=pl.CostEstimate(flops=channels * seq_dev, bytes_accessed=4 * w_out.size, transcendentals=0),
        name="prepare",
    )(*(pltpu.with_memory_space_constraint(x, pltpu.HBM) for x in (key_k, value_v, filter_taps, w_out)))


def gate_kernel(conv_ref, *refs):
    gates, out_ref = refs[:-1], refs[-1]
    blocks, chips, share, _ = conv_ref.shape
    channels = blocks * share
    row = lax.axis_index("tp") // CORES
    for step, gate_ref in enumerate(gates):
        other = (row + chips - step) % chips
        for place, block in enumerate(ctx_order(blocks)):
            rows = pl.ds(block * share, share)
            gated = gate_ref[rows, :].astype(jnp.float32) * conv_ref[place, chips - 1 - other].astype(jnp.float32)
            out_ref[pl.ds(step * channels + block * share, share), :] = gated.astype(jnp.bfloat16)


def gate(convolved, gates):
    blocks, chips, share, seq_dev = convolved.shape
    return pl.pallas_call(
        gate_kernel,
        out_shape=pltpu.VMEM((chips * blocks * share, seq_dev), jnp.bfloat16),
        in_specs=[pl.BlockSpec(memory_space=pltpu.VMEM)] * (1 + chips),
        out_specs=pl.BlockSpec(memory_space=pltpu.VMEM),
        compiler_params=pltpu.CompilerParams(vmem_limit_bytes=8 * 2**20),
        name="gate",
    )(convolved, *(pltpu.with_memory_space_constraint(x, pltpu.VMEM) for x in gates))


def project_own_kernel(gated_ref, *refs):
    *weights, sum_ref, turned_ref = refs
    mine, others = weights[: len(weights) // CORES], weights[len(weights) // CORES :]
    channels = weights[0].shape[0]
    total = None
    for place, weight_ref in enumerate(mine):
        term = lax.dot_general(
            weight_ref[...],
            gated_ref[pl.ds(place * channels, channels), :],
            (((0,), (0,)), ((), ())),
            preferred_element_type=jnp.float32,
        )
        total = term if total is None else total + term
    sum_ref[...] = total
    for place, weight_ref in enumerate(others):
        turned_ref[:, pl.ds(place * channels, channels)] = weight_ref[...].T


def project_other_kernel(gated_ref, sum_ref, turned_ref, out_ref, held, sems):
    parts = sems.shape[0]
    count = out_ref.shape[0] // parts
    copies = []
    for part in range(parts):
        rows = pl.ds(part * count, count)
        term = jnp.dot(turned_ref[rows, :], gated_ref[...], preferred_element_type=jnp.float32)
        held[rows, :] = (sum_ref[rows, :] + term).astype(jnp.bfloat16)
        copies.append(pltpu.make_async_copy(held.at[rows, :], out_ref.at[rows, :], sems.at[part]))
        copies[-1].start()
    for copy in copies:
        copy.wait()


def project(gated_vals, others, weights):
    channels, feats = weights[0].shape
    rows, seq_dev = gated_vals.shape
    vmem = pl.BlockSpec(memory_space=pltpu.VMEM)
    cost = pl.CostEstimate(
        flops=2 * rows * feats * seq_dev, bytes_accessed=2 * rows * (feats + seq_dev), transcendentals=0
    )
    so_far, turned = pl.pallas_call(
        project_own_kernel,
        out_shape=[
            jax.ShapeDtypeStruct((feats, seq_dev), jnp.float32),
            jax.ShapeDtypeStruct((feats, rows), jnp.bfloat16),
        ],
        in_specs=[vmem] * (1 + len(weights)),
        out_specs=[vmem] * 2,
        compiler_params=pltpu.CompilerParams(vmem_limit_bytes=16 * 2**20),
        cost_estimate=cost,
        name="project_own",
    )(gated_vals, *weights)
    return pl.pallas_call(
        project_other_kernel,
        out_shape=jax.ShapeDtypeStruct((feats, seq_dev), jnp.bfloat16),
        in_specs=[vmem] * 3,
        out_specs=pl.BlockSpec(memory_space=pltpu.HBM),
        scratch_shapes=[pltpu.VMEM((feats, seq_dev), jnp.bfloat16), pltpu.SemaphoreType.DMA((PARTS,))],
        compiler_params=pltpu.CompilerParams(vmem_limit_bytes=16 * 2**20),
        cost_estimate=cost,
        name="project_other",
    )(others, so_far, turned)


def body(gate_q, key_k, value_v, filter_taps, skip_bias, w_out):
    channels, seq_dev = key_k.shape
    shards = lax.axis_size("ctx")
    tp = lax.axis_size("tp")
    me = lax.axis_index("tp")
    chips = tp // CORES
    feats = w_out.shape[1] // tp

    def exchange(array, step):
        return lax.ppermute(array, "tp", [(i, partner(i, step, tp)) for i in range(tp)])

    pieces, *cuts = prepare(key_k, value_v, filter_taps, w_out, shards, tp)
    for step in exchanges(tp)[len(cuts) :]:
        cuts.append(lax.dynamic_slice_in_dim(w_out, partner(me, step, tp) * feats, feats, 1))
    weights = [exchange(cut, step) for cut, step in zip(cuts, exchanges(tp))]
    gates = [gate_q] + [exchange(gate_q, (step, 0)) for step in range(1, chips)]

    pieces, arrived = lax.optimization_barrier((pieces, gates[1:]))
    gates = [gate_q, *arrived]
    order = ctx_order(shards)
    pieces = lax.all_to_all(pieces, "ctx", split_axis=0, concat_axis=0, tiled=True, axis_index_groups=[order])
    convolved = convolve(pieces, skip_bias.reshape(channels, 1), chips)
    convolved, weights[0] = lax.optimization_barrier((convolved, weights[0]))
    convolved = lax.all_to_all(
        convolved.reshape(shards * chips, channels // shards, seq_dev),
        ("ctx", "tp"),
        split_axis=0,
        concat_axis=0,
        tiled=True,
        axis_index_groups=[
            [shard * tp + chip * CORES + core for shard in order for chip in reversed(range(chips))] for core in range(CORES)
        ],
    )
    own = lax.dynamic_slice_in_dim(w_out, me * feats, feats, 1)
    convolved, own, weights = lax.optimization_barrier((convolved, own, weights))
    gated_vals = gate(convolved.reshape(shards, chips, channels // shards, seq_dev), gates)
    others = exchange(gated_vals, (0, 1))
    blocks = dict(zip([(0, 0)] + exchanges(tp), [own, *weights]))
    ordered = [blocks[chip, core] for core in range(CORES) for chip in range(chips)]
    return project(gated_vals, others, ordered)


def solution(mesh):
    return jax.shard_map(
        body,
        mesh=mesh,
        in_specs=(P("tp", "ctx"), P("tp", "ctx"), P("tp", "ctx"), P("tp", "ctx"), P("tp"), P("tp", None)),
        out_specs=P("tp", "ctx"),
        check_vma=False,
    )
```

```python
import jax
import jax.numpy as jnp
from jax import lax
from jax.experimental import pallas as pl
from jax.experimental.pallas import tpu as pltpu
from jax.sharding import PartitionSpec as P

LANES = 128
PACK = 16
SUB = 16
PHASES = LANES // SUB
PARTS = 4
CORES = 2


def ctx_order(shards):
    middle = shards // 2
    return [middle] + [shard for shard in range(shards) if shard != middle]


def pitches(lines):
    pad = lines - PHASES
    return pad, (pad + lines) | 1, lines | 1


def conv_kernel(x_ref, bias_ref, y_ref, taps, rows, sums):
    blocks, _, chans, seq_dev = x_ref.shape
    halves = seq_dev // LANES
    place = ctx_order(blocks).index
    lines = blocks * halves
    length = lines * LANES
    pad, row_pitch, sum_pitch = pitches(lines)

    taps[:, pl.ds(0, LANES)] = jnp.zeros((chans, LANES), jnp.float32)
    for phase in range(PHASES):
        for chan in range(chans):
            rows[phase, pl.ds(chan * row_pitch, pad), :] = jnp.zeros((pad, LANES), jnp.float32)
    size = 8 if chans % 8 == 0 else chans
    lane = lax.broadcasted_iota(jnp.int32, (size, LANES), 1)
    bits = PHASES.bit_length() - 1
    odd = [lane // (SUB << bit) % 2 == 1 for bit in range(bits)]
    for begin in range(0, chans, size):
        history = [[[jnp.zeros((size, LANES), jnp.float32)] * PHASES] * (1 << bit) for bit in range(bits)]
        for line in range(lines):
            block, half = divmod(line, halves)
            fresh = x_ref[place(block), 0, pl.ds(begin, size), pl.ds(half * LANES, LANES)].astype(jnp.float32)
            level = [fresh] + [pltpu.roll(fresh, SUB * turn, axis=1) for turn in range(1, PHASES)]
            for bit in range(bits):
                step = 1 << bit
                past = history[bit][0]
                history[bit] = history[bit][1:] + [level]
                level = [jnp.where(odd[bit], past[(turn + step) % PHASES], level[turn]) for turn in range(PHASES)]
            for phase in range(PHASES):
                rows[phase, pl.ds(begin * row_pitch + pad + line, size, stride=row_pitch), :] = level[-phase % PHASES]
    for line in range(lines):
        block, half = divmod(line, halves)
        taps[:, pl.ds(LANES + line * LANES, LANES)] = x_ref[place(block), 1, :, pl.ds(half * LANES, LANES)].astype(jnp.float32)

    def channel(chan, _):
        wide = jnp.broadcast_to(taps[pl.ds(chan, 1), :], (PACK, LANES + length))
        skew = pltpu.roll(wide, 0, 1, stride=1, stride_axis=0).astype(jnp.bfloat16)
        toeplitz = jnp.concatenate([skew[:, (line + 1) * LANES : (line + 2) * LANES] for line in range(lines)], 0)
        base = chan * row_pitch + pad
        left = jnp.concatenate(
            [
                jnp.concatenate(
                    [
                        rows[phase, pl.ds(base - PHASES * step, lines), :].astype(jnp.bfloat16)
                        for step in range(lines // PHASES)
                    ],
                    1,
                )
                for phase in range(PHASES)
            ],
            0,
        )
        total = jnp.dot(left, toeplitz, preferred_element_type=jnp.float32)
        for phase in range(PHASES):
            sums[phase, pl.ds(chan * sum_pitch, lines), :] = total[phase * lines : (phase + 1) * lines]
        return 0

    lax.fori_loop(0, chans, channel, 0, unroll=True)

    first = pl.multiple_of(lax.axis_index("ctx") * chans, chans)
    size = PACK if chans % PACK == 0 else chans
    lane = lax.broadcasted_iota(jnp.int32, (size, LANES), 1)
    for begin in range(0, chans, size):
        part = pl.ds(begin, size)
        bias = jnp.broadcast_to(bias_ref[pl.ds(first + begin, size), :], (size, LANES))
        older = [jnp.zeros((size, LANES), jnp.float32)] * PHASES
        for line in range(lines):
            block, half = divmod(line, halves)
            cut = pl.ds(half * LANES, LANES)
            now = [sums[phase, pl.ds(begin * sum_pitch + line, size, stride=sum_pitch), :] for phase in range(PHASES)]
            value = now[0] + bias * x_ref[place(block), 0, part, cut].astype(jnp.float32)
            for phase in range(1, PHASES):
                mixed = jnp.where(lane < LANES - SUB * phase, now[phase], older[phase])
                value = value + pltpu.roll(mixed, SUB * phase, axis=1)
            older = now
            for copy in range(y_ref.shape[1]):
                y_ref[place(block), copy, part, cut] = value.astype(jnp.bfloat16)


def convolve(pieces, bias, copies):
    blocks, _, chans, seq_dev = pieces.shape
    lines = blocks * seq_dev // LANES
    _, row_pitch, sum_pitch = pitches(lines)
    return pl.pallas_call(
        conv_kernel,
        out_shape=jax.ShapeDtypeStruct((blocks, copies, chans, seq_dev), jnp.bfloat16),
        in_specs=[pl.BlockSpec(memory_space=pltpu.VMEM)] * 2,
        out_specs=pl.BlockSpec(memory_space=pltpu.VMEM),
        scratch_shapes=[
            pltpu.VMEM((chans, LANES + lines * LANES), jnp.float32),
            pltpu.VMEM((PHASES, chans * row_pitch, LANES), jnp.float32),
            pltpu.VMEM((PHASES, chans * sum_pitch, LANES), jnp.float32),
        ],
        compiler_params=pltpu.CompilerParams(vmem_limit_bytes=16 * 2**20),
        cost_estimate=pl.CostEstimate(flops=1, bytes_accessed=1, transcendentals=0),
        name="toeplitz_conv",
    )(pieces, bias)


def partner(me, step, tp):
    chips, other = step
    return (me // CORES + chips) % (tp // CORES) * CORES + (me % CORES + other) % CORES


def source(me, step, tp):
    chips, other = step
    return (me // CORES + tp // CORES - chips) % (tp // CORES) * CORES + (me % CORES + CORES - other) % CORES


def exchanges(tp):
    steps = [(chips, other) for chips in range(tp // CORES) for other in range(CORES)][1:]
    early = (tp // CORES // 2, 0)
    return [early] + [step for step in reversed(steps) if step != early]


def prepare_kernel(key_ref, value_ref, taps_ref, w_ref, pieces_ref, *refs):
    shards, _, share, _ = pieces_ref.shape
    tp = lax.axis_size("tp")
    feats = w_ref.shape[1] // tp
    me = lax.axis_index("tp")
    plan = exchanges(tp)[: len(refs) - 5]
    cuts, (key, value, taps, in_sems, sems) = refs[: len(plan)], refs[len(plan) :]
    loads = []
    for place, (ref, held) in enumerate(((key_ref, key), (value_ref, value), (taps_ref, taps))):
        loads.append(pltpu.make_async_copy(ref, held, in_sems.at[place]))
        loads[-1].start()
    copies = []
    for place, step in enumerate(plan):
        column = pl.multiple_of(partner(me, step, tp) * feats, LANES)
        cut = w_ref.at[:, pl.ds(column, feats)]
        copies.append(pltpu.make_async_copy(cut, cuts[place], sems.at[place]))
        copies[-1].start()
    for load in loads:
        load.wait()
    for place, shard in enumerate(ctx_order(shards)):
        rows = pl.ds(shard * share, share)
        signal = key[rows, :].astype(jnp.float32) * value[rows, :].astype(jnp.float32)
        pieces_ref[place, 0] = signal.astype(jnp.bfloat16)
        pieces_ref[place, 1] = taps[rows, :].astype(jnp.bfloat16)
    for copy in copies:
        copy.wait()


def prepare(key_k, value_v, filter_taps, w_out, shards, tp):
    channels, seq_dev = key_k.shape
    feats = w_out.shape[1] // tp
    plan = exchanges(tp)[:1]
    vmem, hbm = pl.BlockSpec(memory_space=pltpu.VMEM), pl.BlockSpec(memory_space=pltpu.HBM)
    return pl.pallas_call(
        prepare_kernel,
        out_shape=[pltpu.VMEM((shards, 2, channels // shards, seq_dev), jnp.bfloat16)]
        + [pltpu.VMEM((channels, feats), jnp.bfloat16)] * len(plan),
        in_specs=[hbm, hbm, hbm, hbm],
        out_specs=[vmem] * (1 + len(plan)),
        scratch_shapes=[
            pltpu.VMEM(key_k.shape, key_k.dtype),
            pltpu.VMEM(value_v.shape, value_v.dtype),
            pltpu.VMEM(filter_taps.shape, filter_taps.dtype),
            pltpu.SemaphoreType.DMA((3,)),
            pltpu.SemaphoreType.DMA((len(plan),)),
        ],
        compiler_params=pltpu.CompilerParams(vmem_limit_bytes=8 * 2**20),
        cost_estimate=pl.CostEstimate(flops=channels * seq_dev, bytes_accessed=4 * w_out.size, transcendentals=0),
        name="prepare",
    )(*(pltpu.with_memory_space_constraint(x, pltpu.HBM) for x in (key_k, value_v, filter_taps, w_out)))


def gate_kernel(conv_ref, *refs):
    gates, out_ref = refs[:-1], refs[-1]
    blocks, chips, share, _ = conv_ref.shape
    channels = blocks * share
    row = lax.axis_index("tp") // CORES
    for step, gate_ref in enumerate(gates):
        other = (row + chips - step) % chips
        for place, block in enumerate(ctx_order(blocks)):
            rows = pl.ds(block * share, share)
            gated = gate_ref[rows, :].astype(jnp.float32) * conv_ref[place, chips - 1 - other].astype(jnp.float32)
            out_ref[pl.ds(step * channels + block * share, share), :] = gated.astype(jnp.bfloat16)


def gate(convolved, gates):
    blocks, chips, share, seq_dev = convolved.shape
    return pl.pallas_call(
        gate_kernel,
        out_shape=pltpu.VMEM((chips * blocks * share, seq_dev), jnp.bfloat16),
        in_specs=[pl.BlockSpec(memory_space=pltpu.VMEM)] * (1 + chips),
        out_specs=pl.BlockSpec(memory_space=pltpu.VMEM),
        compiler_params=pltpu.CompilerParams(vmem_limit_bytes=8 * 2**20),
        name="gate",
    )(convolved, *(pltpu.with_memory_space_constraint(x, pltpu.VMEM) for x in gates))


def project_own_kernel(gated_ref, *refs):
    *weights, sum_ref, turned_ref = refs
    mine, others = weights[: len(weights) // CORES], weights[len(weights) // CORES :]
    channels = weights[0].shape[0]
    total = None
    for place, weight_ref in enumerate(mine):
        term = lax.dot_general(
            weight_ref[...],
            gated_ref[pl.ds(place * channels, channels), :],
            (((0,), (0,)), ((), ())),
            preferred_element_type=jnp.float32,
        )
        total = term if total is None else total + term
    sum_ref[...] = total
    for place, weight_ref in enumerate(others):
        turned_ref[:, pl.ds(place * channels, channels)] = weight_ref[...].T


def project_other_kernel(gated_ref, sum_ref, turned_ref, out_ref, held, sems):
    parts = sems.shape[0]
    count = out_ref.shape[0] // parts
    copies = []
    for part in range(parts):
        rows = pl.ds(part * count, count)
        term = jnp.dot(turned_ref[rows, :], gated_ref[...], preferred_element_type=jnp.float32)
        held[rows, :] = (sum_ref[rows, :] + term).astype(jnp.bfloat16)
        copies.append(pltpu.make_async_copy(held.at[rows, :], out_ref.at[rows, :], sems.at[part]))
        copies[-1].start()
    for copy in copies:
        copy.wait()


def project(gated_vals, others, weights):
    channels, feats = weights[0].shape
    rows, seq_dev = gated_vals.shape
    vmem = pl.BlockSpec(memory_space=pltpu.VMEM)
    cost = pl.CostEstimate(
        flops=2 * rows * feats * seq_dev, bytes_accessed=2 * rows * (feats + seq_dev), transcendentals=0
    )
    so_far, turned = pl.pallas_call(
        project_own_kernel,
        out_shape=[
            jax.ShapeDtypeStruct((feats, seq_dev), jnp.float32),
            jax.ShapeDtypeStruct((feats, rows), jnp.bfloat16),
        ],
        in_specs=[vmem] * (1 + len(weights)),
        out_specs=[vmem] * 2,
        compiler_params=pltpu.CompilerParams(vmem_limit_bytes=16 * 2**20),
        cost_estimate=cost,
        name="project_own",
    )(gated_vals, *weights)
    return pl.pallas_call(
        project_other_kernel,
        out_shape=jax.ShapeDtypeStruct((feats, seq_dev), jnp.bfloat16),
        in_specs=[vmem] * 3,
        out_specs=pl.BlockSpec(memory_space=pltpu.HBM),
        scratch_shapes=[pltpu.VMEM((feats, seq_dev), jnp.bfloat16), pltpu.SemaphoreType.DMA((PARTS,))],
        compiler_params=pltpu.CompilerParams(vmem_limit_bytes=16 * 2**20),
        cost_estimate=cost,
        name="project_other",
    )(others, so_far, turned)


def body(gate_q, key_k, value_v, filter_taps, skip_bias, w_out):
    channels, seq_dev = key_k.shape
    shards = lax.axis_size("ctx")
    tp = lax.axis_size("tp")
    me = lax.axis_index("tp")
    chips = tp // CORES
    feats = w_out.shape[1] // tp

    def exchange(array, step):
        return lax.ppermute(array, "tp", [(i, partner(i, step, tp)) for i in range(tp)])

    pieces, *cuts = prepare(key_k, value_v, filter_taps, w_out, shards, tp)
    for step in exchanges(tp)[len(cuts) :]:
        cuts.append(lax.dynamic_slice_in_dim(w_out, partner(me, step, tp) * feats, feats, 1))
    weights = [exchange(cut, step) for cut, step in zip(cuts, exchanges(tp))]
    gates = [gate_q] + [exchange(gate_q, (step, 0)) for step in range(1, chips)]

    pieces, arrived = lax.optimization_barrier((pieces, gates[1:]))
    gates = [gate_q, *arrived]
    order = ctx_order(shards)
    pieces = lax.all_to_all(pieces, "ctx", split_axis=0, concat_axis=0, tiled=True, axis_index_groups=[order])
    convolved = convolve(pieces, skip_bias.reshape(channels, 1), chips)
    own = lax.dynamic_slice_in_dim(w_out, me * feats, feats, 1)
    convolved, own, weights[0] = lax.optimization_barrier((convolved, own, weights[0]))
    convolved = lax.all_to_all(
        convolved.reshape(shards * chips, channels // shards, seq_dev),
        ("ctx", "tp"),
        split_axis=0,
        concat_axis=0,
        tiled=True,
        axis_index_groups=[
            [shard * tp + chip * CORES + core for shard in order for chip in reversed(range(chips))] for core in range(CORES)
        ],
    )
    gated_vals = gate(convolved.reshape(shards, chips, channels // shards, seq_dev), gates)
    gated_vals, weights = lax.optimization_barrier((gated_vals, weights))
    others = exchange(gated_vals, (0, 1))
    blocks = dict(zip([(0, 0)] + exchanges(tp), [own, *weights]))
    ordered = [blocks[chip, core] for core in range(CORES) for chip in range(chips)]
    return project(gated_vals, others, ordered)


def solution(mesh):
    return jax.shard_map(
        body,
        mesh=mesh,
        in_specs=(P("tp", "ctx"), P("tp", "ctx"), P("tp", "ctx"), P("tp", "ctx"), P("tp"), P("tp", None)),
        out_specs=P("tp", "ctx"),
        check_vma=False,
    )
```

```python
import jax
import jax.numpy as jnp
from jax import lax
from jax.experimental import pallas as pl
from jax.experimental.pallas import tpu as pltpu
from jax.sharding import PartitionSpec as P

LANES = 128
PACK = 16
SUB = 16
PHASES = LANES // SUB
PARTS = 4
CORES = 2


def ctx_order(shards):
    middle = shards // 2
    return [middle] + [shard for shard in range(shards) if shard != middle]


def pitches(lines):
    pad = lines - PHASES
    return pad, (pad + lines) | 1, lines | 1


def conv_kernel(x_ref, bias_ref, y_ref, taps, rows, sums):
    blocks, _, chans, seq_dev = x_ref.shape
    halves = seq_dev // LANES
    place = ctx_order(blocks).index
    lines = blocks * halves
    length = lines * LANES
    pad, row_pitch, sum_pitch = pitches(lines)

    taps[:, pl.ds(0, LANES)] = jnp.zeros((chans, LANES), jnp.float32)
    for phase in range(PHASES):
        for chan in range(chans):
            rows[phase, pl.ds(chan * row_pitch, pad), :] = jnp.zeros((pad, LANES), jnp.float32)
    size = 8 if chans % 8 == 0 else chans
    lane = lax.broadcasted_iota(jnp.int32, (size, LANES), 1)
    bits = PHASES.bit_length() - 1
    odd = [lane // (SUB << bit) % 2 == 1 for bit in range(bits)]
    for begin in range(0, chans, size):
        history = [[[jnp.zeros((size, LANES), jnp.float32)] * PHASES] * (1 << bit) for bit in range(bits)]
        for line in range(lines):
            block, half = divmod(line, halves)
            fresh = x_ref[place(block), 0, pl.ds(begin, size), pl.ds(half * LANES, LANES)].astype(jnp.float32)
            level = [fresh] + [pltpu.roll(fresh, SUB * turn, axis=1) for turn in range(1, PHASES)]
            for bit in range(bits):
                step = 1 << bit
                past = history[bit][0]
                history[bit] = history[bit][1:] + [level]
                level = [jnp.where(odd[bit], past[(turn + step) % PHASES], level[turn]) for turn in range(PHASES)]
            for phase in range(PHASES):
                rows[phase, pl.ds(begin * row_pitch + pad + line, size, stride=row_pitch), :] = level[-phase % PHASES]
    for line in range(lines):
        block, half = divmod(line, halves)
        taps[:, pl.ds(LANES + line * LANES, LANES)] = x_ref[place(block), 1, :, pl.ds(half * LANES, LANES)].astype(jnp.float32)

    def channel(chan, _):
        wide = jnp.broadcast_to(taps[pl.ds(chan, 1), :], (PACK, LANES + length))
        skew = pltpu.roll(wide, 0, 1, stride=1, stride_axis=0).astype(jnp.bfloat16)
        toeplitz = jnp.concatenate([skew[:, (line + 1) * LANES : (line + 2) * LANES] for line in range(lines)], 0)
        base = chan * row_pitch + pad
        left = jnp.concatenate(
            [
                jnp.concatenate(
                    [
                        rows[phase, pl.ds(base - PHASES * step, lines), :].astype(jnp.bfloat16)
                        for step in range(lines // PHASES)
                    ],
                    1,
                )
                for phase in range(PHASES)
            ],
            0,
        )
        total = jnp.dot(left, toeplitz, preferred_element_type=jnp.float32)
        for phase in range(PHASES):
            sums[phase, pl.ds(chan * sum_pitch, lines), :] = total[phase * lines : (phase + 1) * lines]
        return 0

    lax.fori_loop(0, chans, channel, 0, unroll=True)

    first = pl.multiple_of(lax.axis_index("ctx") * chans, chans)
    size = PACK if chans % PACK == 0 else chans
    lane = lax.broadcasted_iota(jnp.int32, (size, LANES), 1)
    for begin in range(0, chans, size):
        part = pl.ds(begin, size)
        bias = jnp.broadcast_to(bias_ref[pl.ds(first + begin, size), :], (size, LANES))
        older = [jnp.zeros((size, LANES), jnp.float32)] * PHASES
        for line in range(lines):
            block, half = divmod(line, halves)
            cut = pl.ds(half * LANES, LANES)
            now = [sums[phase, pl.ds(begin * sum_pitch + line, size, stride=sum_pitch), :] for phase in range(PHASES)]
            value = now[0] + bias * x_ref[place(block), 0, part, cut].astype(jnp.float32)
            for phase in range(1, PHASES):
                mixed = jnp.where(lane < LANES - SUB * phase, now[phase], older[phase])
                value = value + pltpu.roll(mixed, SUB * phase, axis=1)
            older = now
            for copy in range(y_ref.shape[1]):
                y_ref[place(block), copy, part, cut] = value.astype(jnp.bfloat16)


def convolve(pieces, bias, copies):
    blocks, _, chans, seq_dev = pieces.shape
    lines = blocks * seq_dev // LANES
    _, row_pitch, sum_pitch = pitches(lines)
    return pl.pallas_call(
        conv_kernel,
        out_shape=jax.ShapeDtypeStruct((blocks, copies, chans, seq_dev), jnp.bfloat16),
        in_specs=[pl.BlockSpec(memory_space=pltpu.VMEM)] * 2,
        out_specs=pl.BlockSpec(memory_space=pltpu.VMEM),
        scratch_shapes=[
            pltpu.VMEM((chans, LANES + lines * LANES), jnp.float32),
            pltpu.VMEM((PHASES, chans * row_pitch, LANES), jnp.float32),
            pltpu.VMEM((PHASES, chans * sum_pitch, LANES), jnp.float32),
        ],
        compiler_params=pltpu.CompilerParams(vmem_limit_bytes=16 * 2**20),
        cost_estimate=pl.CostEstimate(flops=1, bytes_accessed=1, transcendentals=0),
        name="toeplitz_conv",
    )(pieces, bias)


def partner(me, step, tp):
    chips, other = step
    return (me // CORES + chips) % (tp // CORES) * CORES + (me % CORES + other) % CORES


def source(me, step, tp):
    chips, other = step
    return (me // CORES + tp // CORES - chips) % (tp // CORES) * CORES + (me % CORES + CORES - other) % CORES


def exchanges(tp):
    steps = [(chips, other) for chips in range(tp // CORES) for other in range(CORES)][1:]
    early = (tp // CORES // 2, 0)
    return [early] + [step for step in steps if step != early]


def prepare_kernel(key_ref, value_ref, taps_ref, w_ref, pieces_ref, *refs):
    shards, _, share, _ = pieces_ref.shape
    tp = lax.axis_size("tp")
    feats = w_ref.shape[1] // tp
    me = lax.axis_index("tp")
    plan = exchanges(tp)[: len(refs) - 5]
    cuts, (key, value, taps, in_sems, sems) = refs[: len(plan)], refs[len(plan) :]
    loads = []
    for place, (ref, held) in enumerate(((key_ref, key), (value_ref, value), (taps_ref, taps))):
        loads.append(pltpu.make_async_copy(ref, held, in_sems.at[place]))
        loads[-1].start()
    copies = []
    for place, step in enumerate(plan):
        column = pl.multiple_of(partner(me, step, tp) * feats, LANES)
        cut = w_ref.at[:, pl.ds(column, feats)]
        copies.append(pltpu.make_async_copy(cut, cuts[place], sems.at[place]))
        copies[-1].start()
    for load in loads:
        load.wait()
    for place, shard in enumerate(ctx_order(shards)):
        rows = pl.ds(shard * share, share)
        signal = key[rows, :].astype(jnp.float32) * value[rows, :].astype(jnp.float32)
        pieces_ref[place, 0] = signal.astype(jnp.bfloat16)
        pieces_ref[place, 1] = taps[rows, :].astype(jnp.bfloat16)
    for copy in copies:
        copy.wait()


def prepare(key_k, value_v, filter_taps, w_out, shards, tp):
    channels, seq_dev = key_k.shape
    feats = w_out.shape[1] // tp
    plan = exchanges(tp)[:1]
    vmem, hbm = pl.BlockSpec(memory_space=pltpu.VMEM), pl.BlockSpec(memory_space=pltpu.HBM)
    return pl.pallas_call(
        prepare_kernel,
        out_shape=[pltpu.VMEM((shards, 2, channels // shards, seq_dev), jnp.bfloat16)]
        + [pltpu.VMEM((channels, feats), jnp.bfloat16)] * len(plan),
        in_specs=[hbm, hbm, hbm, hbm],
        out_specs=[vmem] * (1 + len(plan)),
        scratch_shapes=[
            pltpu.VMEM(key_k.shape, key_k.dtype),
            pltpu.VMEM(value_v.shape, value_v.dtype),
            pltpu.VMEM(filter_taps.shape, filter_taps.dtype),
            pltpu.SemaphoreType.DMA((3,)),
            pltpu.SemaphoreType.DMA((len(plan),)),
        ],
        compiler_params=pltpu.CompilerParams(vmem_limit_bytes=8 * 2**20),
        cost_estimate=pl.CostEstimate(flops=channels * seq_dev, bytes_accessed=4 * w_out.size, transcendentals=0),
        name="prepare",
    )(*(pltpu.with_memory_space_constraint(x, pltpu.HBM) for x in (key_k, value_v, filter_taps, w_out)))


def gate_kernel(conv_ref, *refs):
    gates, out_ref = refs[:-1], refs[-1]
    blocks, chips, share, _ = conv_ref.shape
    channels = blocks * share
    row = lax.axis_index("tp") // CORES
    for step, gate_ref in enumerate(gates):
        other = (row + chips - step) % chips
        for place, block in enumerate(ctx_order(blocks)):
            rows = pl.ds(block * share, share)
            gated = gate_ref[rows, :].astype(jnp.float32) * conv_ref[place, chips - 1 - other].astype(jnp.float32)
            out_ref[pl.ds(step * channels + block * share, share), :] = gated.astype(jnp.bfloat16)


def gate(convolved, gates):
    blocks, chips, share, seq_dev = convolved.shape
    return pl.pallas_call(
        gate_kernel,
        out_shape=pltpu.VMEM((chips * blocks * share, seq_dev), jnp.bfloat16),
        in_specs=[pl.BlockSpec(memory_space=pltpu.VMEM)] * (1 + chips),
        out_specs=pl.BlockSpec(memory_space=pltpu.VMEM),
        compiler_params=pltpu.CompilerParams(vmem_limit_bytes=8 * 2**20),
        name="gate",
    )(convolved, *(pltpu.with_memory_space_constraint(x, pltpu.VMEM) for x in gates))


def project_own_kernel(gated_ref, *refs):
    *weights, sum_ref, turned_ref = refs
    mine, others = weights[: len(weights) // CORES], weights[len(weights) // CORES :]
    channels = weights[0].shape[0]
    total = None
    for place, weight_ref in enumerate(mine):
        term = lax.dot_general(
            weight_ref[...],
            gated_ref[pl.ds(place * channels, channels), :],
            (((0,), (0,)), ((), ())),
            preferred_element_type=jnp.float32,
        )
        total = term if total is None else total + term
    sum_ref[...] = total
    for place, weight_ref in enumerate(others):
        turned_ref[:, pl.ds(place * channels, channels)] = weight_ref[...].T


def project_other_kernel(gated_ref, sum_ref, turned_ref, out_ref, held, sems):
    parts = sems.shape[0]
    count = out_ref.shape[0] // parts
    copies = []
    for part in range(parts):
        rows = pl.ds(part * count, count)
        term = jnp.dot(turned_ref[rows, :], gated_ref[...], preferred_element_type=jnp.float32)
        held[rows, :] = (sum_ref[rows, :] + term).astype(jnp.bfloat16)
        copies.append(pltpu.make_async_copy(held.at[rows, :], out_ref.at[rows, :], sems.at[part]))
        copies[-1].start()
    for copy in copies:
        copy.wait()


def project(gated_vals, others, weights):
    channels, feats = weights[0].shape
    rows, seq_dev = gated_vals.shape
    vmem = pl.BlockSpec(memory_space=pltpu.VMEM)
    cost = pl.CostEstimate(
        flops=2 * rows * feats * seq_dev, bytes_accessed=2 * rows * (feats + seq_dev), transcendentals=0
    )
    so_far, turned = pl.pallas_call(
        project_own_kernel,
        out_shape=[
            jax.ShapeDtypeStruct((feats, seq_dev), jnp.float32),
            jax.ShapeDtypeStruct((feats, rows), jnp.bfloat16),
        ],
        in_specs=[vmem] * (1 + len(weights)),
        out_specs=[vmem] * 2,
        compiler_params=pltpu.CompilerParams(vmem_limit_bytes=16 * 2**20),
        cost_estimate=cost,
        name="project_own",
    )(gated_vals, *weights)
    return pl.pallas_call(
        project_other_kernel,
        out_shape=jax.ShapeDtypeStruct((feats, seq_dev), jnp.bfloat16),
        in_specs=[vmem] * 3,
        out_specs=pl.BlockSpec(memory_space=pltpu.HBM),
        scratch_shapes=[pltpu.VMEM((feats, seq_dev), jnp.bfloat16), pltpu.SemaphoreType.DMA((PARTS,))],
        compiler_params=pltpu.CompilerParams(vmem_limit_bytes=16 * 2**20),
        cost_estimate=cost,
        name="project_other",
    )(others, so_far, turned)


def body(gate_q, key_k, value_v, filter_taps, skip_bias, w_out):
    channels, seq_dev = key_k.shape
    shards = lax.axis_size("ctx")
    tp = lax.axis_size("tp")
    me = lax.axis_index("tp")
    chips = tp // CORES
    feats = w_out.shape[1] // tp

    def exchange(array, step):
        return lax.ppermute(array, "tp", [(i, partner(i, step, tp)) for i in range(tp)])

    pieces, *cuts = prepare(key_k, value_v, filter_taps, w_out, shards, tp)
    for step in exchanges(tp)[len(cuts) :]:
        cuts.append(lax.dynamic_slice_in_dim(w_out, partner(me, step, tp) * feats, feats, 1))
    weights = [exchange(cut, step) for cut, step in zip(cuts, exchanges(tp))]
    gates = [gate_q] + [exchange(gate_q, (step, 0)) for step in range(1, chips)]

    pieces, arrived = lax.optimization_barrier((pieces, gates[1:]))
    gates = [gate_q, *arrived]
    order = ctx_order(shards)
    pieces = lax.all_to_all(pieces, "ctx", split_axis=0, concat_axis=0, tiled=True, axis_index_groups=[order])
    convolved = convolve(pieces, skip_bias.reshape(channels, 1), chips)
    own = lax.dynamic_slice_in_dim(w_out, me * feats, feats, 1)
    convolved, own, weights[0] = lax.optimization_barrier((convolved, own, weights[0]))
    convolved = lax.all_to_all(
        convolved.reshape(shards * chips, channels // shards, seq_dev),
        ("ctx", "tp"),
        split_axis=0,
        concat_axis=0,
        tiled=True,
        axis_index_groups=[
            [shard * tp + chip * CORES + core for shard in order for chip in reversed(range(chips))] for core in range(CORES)
        ],
    )
    gated_vals = gate(convolved.reshape(shards, chips, channels // shards, seq_dev), gates)
    gated_vals, weights = lax.optimization_barrier((gated_vals, weights))
    others = exchange(gated_vals, (0, 1))
    blocks = dict(zip([(0, 0)] + exchanges(tp), [own, *weights]))
    ordered = [blocks[chip, core] for core in range(CORES) for chip in range(chips)]
    return project(gated_vals, others, ordered)


def solution(mesh):
    return jax.shard_map(
        body,
        mesh=mesh,
        in_specs=(P("tp", "ctx"), P("tp", "ctx"), P("tp", "ctx"), P("tp", "ctx"), P("tp"), P("tp", None)),
        out_specs=P("tp", "ctx"),
        check_vma=False,
    )
```

```python
import jax
import jax.numpy as jnp
from jax import lax
from jax.experimental import pallas as pl
from jax.experimental.pallas import tpu as pltpu
from jax.sharding import PartitionSpec as P

LANES = 128
PACK = 16
SUB = 16
PHASES = LANES // SUB
PARTS = 4
CORES = 2


def ctx_order(shards):
    middle = shards // 2
    others = [shard for shard in range(shards) if shard != middle]
    return [middle] + sorted(others, key=lambda shard: -abs(shard - middle))


def pitches(lines):
    pad = lines - PHASES
    return pad, (pad + lines) | 1, lines | 1


def conv_kernel(x_ref, bias_ref, y_ref, taps, rows, sums):
    blocks, _, chans, seq_dev = x_ref.shape
    halves = seq_dev // LANES
    place = ctx_order(blocks).index
    lines = blocks * halves
    length = lines * LANES
    pad, row_pitch, sum_pitch = pitches(lines)

    taps[:, pl.ds(0, LANES)] = jnp.zeros((chans, LANES), jnp.float32)
    for phase in range(PHASES):
        for chan in range(chans):
            rows[phase, pl.ds(chan * row_pitch, pad), :] = jnp.zeros((pad, LANES), jnp.float32)
    size = 8 if chans % 8 == 0 else chans
    lane = lax.broadcasted_iota(jnp.int32, (size, LANES), 1)
    bits = PHASES.bit_length() - 1
    odd = [lane // (SUB << bit) % 2 == 1 for bit in range(bits)]
    for begin in range(0, chans, size):
        history = [[[jnp.zeros((size, LANES), jnp.float32)] * PHASES] * (1 << bit) for bit in range(bits)]
        for line in range(lines):
            block, half = divmod(line, halves)
            fresh = x_ref[place(block), 0, pl.ds(begin, size), pl.ds(half * LANES, LANES)].astype(jnp.float32)
            level = [fresh] + [pltpu.roll(fresh, SUB * turn, axis=1) for turn in range(1, PHASES)]
            for bit in range(bits):
                step = 1 << bit
                past = history[bit][0]
                history[bit] = history[bit][1:] + [level]
                level = [jnp.where(odd[bit], past[(turn + step) % PHASES], level[turn]) for turn in range(PHASES)]
            for phase in range(PHASES):
                rows[phase, pl.ds(begin * row_pitch + pad + line, size, stride=row_pitch), :] = level[-phase % PHASES]
    for line in range(lines):
        block, half = divmod(line, halves)
        taps[:, pl.ds(LANES + line * LANES, LANES)] = x_ref[place(block), 1, :, pl.ds(half * LANES, LANES)].astype(jnp.float32)

    def channel(chan, _):
        wide = jnp.broadcast_to(taps[pl.ds(chan, 1), :], (PACK, LANES + length))
        skew = pltpu.roll(wide, 0, 1, stride=1, stride_axis=0).astype(jnp.bfloat16)
        toeplitz = jnp.concatenate([skew[:, (line + 1) * LANES : (line + 2) * LANES] for line in range(lines)], 0)
        base = chan * row_pitch + pad
        left = jnp.concatenate(
            [
                jnp.concatenate(
                    [
                        rows[phase, pl.ds(base - PHASES * step, lines), :].astype(jnp.bfloat16)
                        for step in range(lines // PHASES)
                    ],
                    1,
                )
                for phase in range(PHASES)
            ],
            0,
        )
        total = jnp.dot(left, toeplitz, preferred_element_type=jnp.float32)
        for phase in range(PHASES):
            sums[phase, pl.ds(chan * sum_pitch, lines), :] = total[phase * lines : (phase + 1) * lines]
        return 0

    lax.fori_loop(0, chans, channel, 0, unroll=True)

    first = pl.multiple_of(lax.axis_index("ctx") * chans, chans)
    size = PACK if chans % PACK == 0 else chans
    lane = lax.broadcasted_iota(jnp.int32, (size, LANES), 1)
    for begin in range(0, chans, size):
        part = pl.ds(begin, size)
        bias = jnp.broadcast_to(bias_ref[pl.ds(first + begin, size), :], (size, LANES))
        older = [jnp.zeros((size, LANES), jnp.float32)] * PHASES
        for line in range(lines):
            block, half = divmod(line, halves)
            cut = pl.ds(half * LANES, LANES)
            now = [sums[phase, pl.ds(begin * sum_pitch + line, size, stride=sum_pitch), :] for phase in range(PHASES)]
            value = now[0] + bias * x_ref[place(block), 0, part, cut].astype(jnp.float32)
            for phase in range(1, PHASES):
                mixed = jnp.where(lane < LANES - SUB * phase, now[phase], older[phase])
                value = value + pltpu.roll(mixed, SUB * phase, axis=1)
            older = now
            for copy in range(y_ref.shape[1]):
                y_ref[place(block), copy, part, cut] = value.astype(jnp.bfloat16)


def convolve(pieces, bias, copies):
    blocks, _, chans, seq_dev = pieces.shape
    lines = blocks * seq_dev // LANES
    _, row_pitch, sum_pitch = pitches(lines)
    return pl.pallas_call(
        conv_kernel,
        out_shape=jax.ShapeDtypeStruct((blocks, copies, chans, seq_dev), jnp.bfloat16),
        in_specs=[pl.BlockSpec(memory_space=pltpu.VMEM)] * 2,
        out_specs=pl.BlockSpec(memory_space=pltpu.VMEM),
        scratch_shapes=[
            pltpu.VMEM((chans, LANES + lines * LANES), jnp.float32),
            pltpu.VMEM((PHASES, chans * row_pitch, LANES), jnp.float32),
            pltpu.VMEM((PHASES, chans * sum_pitch, LANES), jnp.float32),
        ],
        compiler_params=pltpu.CompilerParams(vmem_limit_bytes=16 * 2**20),
        cost_estimate=pl.CostEstimate(flops=1, bytes_accessed=1, transcendentals=0),
        name="toeplitz_conv",
    )(pieces, bias)


def partner(me, step, tp):
    chips, other = step
    return (me // CORES + chips) % (tp // CORES) * CORES + (me % CORES + other) % CORES


def source(me, step, tp):
    chips, other = step
    return (me // CORES + tp // CORES - chips) % (tp // CORES) * CORES + (me % CORES + CORES - other) % CORES


def exchanges(tp):
    steps = [(chips, other) for chips in range(tp // CORES) for other in range(CORES)][1:]
    early = (tp // CORES // 2, 0)
    return [early] + [step for step in steps if step != early]


def prepare_kernel(key_ref, value_ref, taps_ref, w_ref, pieces_ref, *refs):
    shards, _, share, _ = pieces_ref.shape
    tp = lax.axis_size("tp")
    feats = w_ref.shape[1] // tp
    me = lax.axis_index("tp")
    plan = exchanges(tp)[: len(refs) - 5]
    cuts, (key, value, taps, in_sems, sems) = refs[: len(plan)], refs[len(plan) :]
    loads = []
    for place, (ref, held) in enumerate(((key_ref, key), (value_ref, value), (taps_ref, taps))):
        loads.append(pltpu.make_async_copy(ref, held, in_sems.at[place]))
        loads[-1].start()
    copies = []
    for place, step in enumerate(plan):
        column = pl.multiple_of(partner(me, step, tp) * feats, LANES)
        cut = w_ref.at[:, pl.ds(column, feats)]
        copies.append(pltpu.make_async_copy(cut, cuts[place], sems.at[place]))
        copies[-1].start()
    for load in loads:
        load.wait()
    for place, shard in enumerate(ctx_order(shards)):
        rows = pl.ds(shard * share, share)
        signal = key[rows, :].astype(jnp.float32) * value[rows, :].astype(jnp.float32)
        pieces_ref[place, 0] = signal.astype(jnp.bfloat16)
        pieces_ref[place, 1] = taps[rows, :].astype(jnp.bfloat16)
    for copy in copies:
        copy.wait()


def prepare(key_k, value_v, filter_taps, w_out, shards, tp):
    channels, seq_dev = key_k.shape
    feats = w_out.shape[1] // tp
    plan = exchanges(tp)[:1]
    vmem, hbm = pl.BlockSpec(memory_space=pltpu.VMEM), pl.BlockSpec(memory_space=pltpu.HBM)
    return pl.pallas_call(
        prepare_kernel,
        out_shape=[pltpu.VMEM((shards, 2, channels // shards, seq_dev), jnp.bfloat16)]
        + [pltpu.VMEM((channels, feats), jnp.bfloat16)] * len(plan),
        in_specs=[hbm, hbm, hbm, hbm],
        out_specs=[vmem] * (1 + len(plan)),
        scratch_shapes=[
            pltpu.VMEM(key_k.shape, key_k.dtype),
            pltpu.VMEM(value_v.shape, value_v.dtype),
            pltpu.VMEM(filter_taps.shape, filter_taps.dtype),
            pltpu.SemaphoreType.DMA((3,)),
            pltpu.SemaphoreType.DMA((len(plan),)),
        ],
        compiler_params=pltpu.CompilerParams(vmem_limit_bytes=8 * 2**20),
        cost_estimate=pl.CostEstimate(flops=channels * seq_dev, bytes_accessed=4 * w_out.size, transcendentals=0),
        name="prepare",
    )(*(pltpu.with_memory_space_constraint(x, pltpu.HBM) for x in (key_k, value_v, filter_taps, w_out)))


def gate_kernel(conv_ref, *refs):
    gates, out_ref = refs[:-1], refs[-1]
    blocks, chips, share, _ = conv_ref.shape
    channels = blocks * share
    row = lax.axis_index("tp") // CORES
    for step, gate_ref in enumerate(gates):
        other = (row + chips - step) % chips
        for place, block in enumerate(ctx_order(blocks)):
            rows = pl.ds(block * share, share)
            gated = gate_ref[rows, :].astype(jnp.float32) * conv_ref[place, chips - 1 - other].astype(jnp.float32)
            out_ref[pl.ds(step * channels + block * share, share), :] = gated.astype(jnp.bfloat16)


def gate(convolved, gates):
    blocks, chips, share, seq_dev = convolved.shape
    return pl.pallas_call(
        gate_kernel,
        out_shape=pltpu.VMEM((chips * blocks * share, seq_dev), jnp.bfloat16),
        in_specs=[pl.BlockSpec(memory_space=pltpu.VMEM)] * (1 + chips),
        out_specs=pl.BlockSpec(memory_space=pltpu.VMEM),
        compiler_params=pltpu.CompilerParams(vmem_limit_bytes=8 * 2**20),
        name="gate",
    )(convolved, *(pltpu.with_memory_space_constraint(x, pltpu.VMEM) for x in gates))


def project_own_kernel(gated_ref, *refs):
    *weights, sum_ref, turned_ref = refs
    mine, others = weights[: len(weights) // CORES], weights[len(weights) // CORES :]
    channels = weights[0].shape[0]
    total = None
    for place, weight_ref in enumerate(mine):
        term = lax.dot_general(
            weight_ref[...],
            gated_ref[pl.ds(place * channels, channels), :],
            (((0,), (0,)), ((), ())),
            preferred_element_type=jnp.float32,
        )
        total = term if total is None else total + term
    sum_ref[...] = total
    for place, weight_ref in enumerate(others):
        turned_ref[:, pl.ds(place * channels, channels)] = weight_ref[...].T


def project_other_kernel(gated_ref, sum_ref, turned_ref, out_ref, held, sems):
    parts = sems.shape[0]
    count = out_ref.shape[0] // parts
    copies = []
    for part in range(parts):
        rows = pl.ds(part * count, count)
        term = jnp.dot(turned_ref[rows, :], gated_ref[...], preferred_element_type=jnp.float32)
        held[rows, :] = (sum_ref[rows, :] + term).astype(jnp.bfloat16)
        copies.append(pltpu.make_async_copy(held.at[rows, :], out_ref.at[rows, :], sems.at[part]))
        copies[-1].start()
    for copy in copies:
        copy.wait()


def project(gated_vals, others, weights):
    channels, feats = weights[0].shape
    rows, seq_dev = gated_vals.shape
    vmem = pl.BlockSpec(memory_space=pltpu.VMEM)
    cost = pl.CostEstimate(
        flops=2 * rows * feats * seq_dev, bytes_accessed=2 * rows * (feats + seq_dev), transcendentals=0
    )
    so_far, turned = pl.pallas_call(
        project_own_kernel,
        out_shape=[
            jax.ShapeDtypeStruct((feats, seq_dev), jnp.float32),
            jax.ShapeDtypeStruct((feats, rows), jnp.bfloat16),
        ],
        in_specs=[vmem] * (1 + len(weights)),
        out_specs=[vmem] * 2,
        compiler_params=pltpu.CompilerParams(vmem_limit_bytes=16 * 2**20),
        cost_estimate=cost,
        name="project_own",
    )(gated_vals, *weights)
    return pl.pallas_call(
        project_other_kernel,
        out_shape=jax.ShapeDtypeStruct((feats, seq_dev), jnp.bfloat16),
        in_specs=[vmem] * 3,
        out_specs=pl.BlockSpec(memory_space=pltpu.HBM),
        scratch_shapes=[pltpu.VMEM((feats, seq_dev), jnp.bfloat16), pltpu.SemaphoreType.DMA((PARTS,))],
        compiler_params=pltpu.CompilerParams(vmem_limit_bytes=16 * 2**20),
        cost_estimate=cost,
        name="project_other",
    )(others, so_far, turned)


def body(gate_q, key_k, value_v, filter_taps, skip_bias, w_out):
    channels, seq_dev = key_k.shape
    shards = lax.axis_size("ctx")
    tp = lax.axis_size("tp")
    me = lax.axis_index("tp")
    chips = tp // CORES
    feats = w_out.shape[1] // tp

    def exchange(array, step):
        return lax.ppermute(array, "tp", [(i, partner(i, step, tp)) for i in range(tp)])

    pieces, *cuts = prepare(key_k, value_v, filter_taps, w_out, shards, tp)
    for step in exchanges(tp)[len(cuts) :]:
        cuts.append(lax.dynamic_slice_in_dim(w_out, partner(me, step, tp) * feats, feats, 1))
    weights = [exchange(cut, step) for cut, step in zip(cuts, exchanges(tp))]
    gates = [gate_q] + [exchange(gate_q, (step, 0)) for step in range(1, chips)]

    pieces, arrived = lax.optimization_barrier((pieces, gates[1:]))
    gates = [gate_q, *arrived]
    order = ctx_order(shards)
    pieces = lax.all_to_all(pieces, "ctx", split_axis=0, concat_axis=0, tiled=True, axis_index_groups=[order])
    convolved = convolve(pieces, skip_bias.reshape(channels, 1), chips)
    own = lax.dynamic_slice_in_dim(w_out, me * feats, feats, 1)
    convolved, own, weights[0] = lax.optimization_barrier((convolved, own, weights[0]))
    convolved = lax.all_to_all(
        convolved.reshape(shards * chips, channels // shards, seq_dev),
        ("ctx", "tp"),
        split_axis=0,
        concat_axis=0,
        tiled=True,
        axis_index_groups=[
            [shard * tp + chip * CORES + core for shard in order for chip in reversed(range(chips))] for core in range(CORES)
        ],
    )
    gated_vals = gate(convolved.reshape(shards, chips, channels // shards, seq_dev), gates)
    gated_vals, weights = lax.optimization_barrier((gated_vals, weights))
    others = exchange(gated_vals, (0, 1))
    blocks = dict(zip([(0, 0)] + exchanges(tp), [own, *weights]))
    ordered = [blocks[chip, core] for core in range(CORES) for chip in range(chips)]
    return project(gated_vals, others, ordered)


def solution(mesh):
    return jax.shard_map(
        body,
        mesh=mesh,
        in_specs=(P("tp", "ctx"), P("tp", "ctx"), P("tp", "ctx"), P("tp", "ctx"), P("tp"), P("tp", None)),
        out_specs=P("tp", "ctx"),
        check_vma=False,
    )
```
